32 devices in a mesh: nodes: 32 (over z, y, x, core).
Axes of the slice: x: 2, y: 2, z: 4, core: 2. Of those that a mesh axis runs over, the one named last changes fastest.
Arguments:
- features: bfloat16 [32768, 128], P('nodes'), may hold values from 0 to 2
- send_lists: int32 [32, 32, 16], P('nodes'), may hold values from 0 to 1023
- hub_rows: int32 [2048], P('nodes'), may hold values from 0 to 1023
- local_tiles: bfloat16 [3072, 128, 128], P('nodes'), may hold values from 0 to 2, as said below
- local_dst: int32 [3072], P('nodes'), may hold values from 0 to 7
- local_src: int32 [3072], P('nodes'), may hold values from 0 to 7
- remote_tiles: bfloat16 [3072, 128, 128], P('nodes'), may hold values from 0 to 2, as said below
- remote_dst: int32 [3072], P('nodes'), may hold values from 0 to 7
- remote_src: int32 [3072], P('nodes'), may hold values from 0 to 3
- hub_tiles: bfloat16 [3072, 128, 128], P('nodes'), may hold values from 0 to 2, as said below
- hub_dst: int32 [3072], P('nodes'), may hold values from 0 to 7
- hub_src: int32 [3072], P('nodes'), may hold values from 0 to 15
- self_one: bfloat16 [128, 256], replicated, may hold values from -0.5 to 0.5
- neigh_one: bfloat16 [128, 256], replicated, may hold values from -0.5 to 0.5
- self_two: bfloat16 [256, 256], replicated, may hold values from -0.375 to 0.375
- neigh_two: bfloat16 [256, 256], replicated, may hold values from -0.375 to 0.375
Outputs:
- embedding: float32 [32768, 256], P('nodes')
The draws below stay inside these ranges and needn't reach their ends.
Inputs may be any that keep to these rules, and one draw needn't show every extreme that they name: `local_tiles`: tile entries are zero or positive edge weights; about one entry in 128 is nonzero. `remote_tiles`: tile entries are zero or positive edge weights; about one entry in 128 is nonzero. `hub_tiles`: tile entries are zero or positive edge weights; about one entry in 128 is nonzero.
All inputs are finite; a program needn't handle non-finite values.
Results may differ from the reference program's by a relative error of at most 0.0033.
Values may be sent and summed in bfloat16 or wider, within the bound.
No kernel may reach another device: no remote copies, remote signals or barrier semaphores. Data moves between devices by JAX's collectives and lax.ppermute only.
A program may use at most 128 MiB of HBM per device.

```python
import jax
import jax.numpy as jnp
from jax import lax

F_IN = 128
HID = 256
BLK = 128
NODE_DEV = 1024
SEND = 16
HUB_DEV = 64
LTILES = 96
RTILES = 96
HTILES = 96
NODES = 32768
HUBS = 2048
REMOTE = 512
N_NODES = 32


def tile_values(key, count, low, high):
    shape = (count, BLK, BLK)
    key_mask, key_value = jax.random.split(key)
    present = jax.random.uniform(key_mask, shape, jnp.float32) < 1.0 / BLK
    weight = jnp.exp(jax.random.uniform(key_value, shape, jnp.float32, jnp.log(low), jnp.log(high)))
    return jnp.where(present, weight, 0.0).astype(jnp.bfloat16)


def level_field(key, row_low, col_low, entry_low):
    key_row, key_col, key_entry = jax.random.split(key, 3)
    row_level = jax.random.uniform(key_row, (NODES, 1), jnp.float32, row_low, 0.69)
    col_level = jax.random.uniform(key_col, (1, F_IN), jnp.float32, col_low, 0.0)
    entry_level = jax.random.uniform(key_entry, (NODES, F_IN), jnp.float32, entry_low, 0.0)
    return jnp.exp(row_level + col_level + entry_level).astype(jnp.bfloat16)


def draw_features(key, part):
    key = jax.random.fold_in(key, 5)
    return level_field(key, -2.0, -1.0, -1.0)


def draw_local_tiles(key, part):
    key = jax.random.fold_in(key, 11)
    return tile_values(key, N_NODES * LTILES, 0.01, 2.0)


def draw_remote_tiles(key, part):
    key = jax.random.fold_in(key, 23)
    return tile_values(key, N_NODES * RTILES, 0.01, 2.0)


def draw_hub_tiles(key, part):
    key = jax.random.fold_in(key, 37)
    return tile_values(key, N_NODES * HTILES, 0.01, 2.0)


def set_ends(drawn, rng, least, largest):
    dims = drawn.shape
    spot = [jax.random.randint(jax.random.fold_in(rng, axis), (), 0, dims[axis]) for axis in range(len(dims))]
    drawn = drawn.at[tuple(spot)].set(least)
    longest = dims.index(max(dims))
    spot[longest] = (spot[longest] + 1) % dims[longest]
    return drawn.at[tuple(spot)].set(largest)


def noise(stream_key, extent, deviation, limit, kind=jnp.bfloat16):
    values = jax.random.normal(stream_key, extent, jnp.float32) * deviation
    return jnp.minimum(jnp.maximum(values, -limit), limit).astype(kind)


def setup_inputs(seed: int = 0) -> dict:
    arg_keys = jax.random.split(jax.random.key(seed), 17)
    return {
        "features": draw_features(jax.random.fold_in(arg_keys[16], 71), 0),
        "send_lists": set_ends(jax.random.randint(arg_keys[1], (N_NODES, N_NODES, SEND), 0, NODE_DEV), jax.random.fold_in(arg_keys[1], 1), 0, NODE_DEV - 1).astype(jnp.int32),
        "hub_rows": set_ends(jax.random.randint(arg_keys[2], (HUBS,), 0, NODE_DEV), jax.random.fold_in(arg_keys[2], 1), 0, NODE_DEV - 1).astype(jnp.int32),
        "local_tiles": draw_local_tiles(jax.random.fold_in(arg_keys[16], 71), 0),
        "local_dst": set_ends(jax.random.randint(arg_keys[4], (N_NODES * LTILES,), 0, NODE_DEV // BLK), jax.random.fold_in(arg_keys[4], 1), 0, (NODE_DEV // BLK) - 1).astype(jnp.int32),
        "local_src": set_ends(jax.random.randint(arg_keys[5], (N_NODES * LTILES,), 0, NODE_DEV // BLK), jax.random.fold_in(arg_keys[5], 1), 0, (NODE_DEV // BLK) - 1).astype(jnp.int32),
        "remote_tiles": draw_remote_tiles(jax.random.fold_in(arg_keys[16], 71), 0),
        "remote_dst": set_ends(jax.random.randint(arg_keys[7], (N_NODES * RTILES,), 0, NODE_DEV // BLK), jax.random.fold_in(arg_keys[7], 1), 0, (NODE_DEV // BLK) - 1).astype(jnp.int32),
        "remote_src": set_ends(jax.random.randint(arg_keys[8], (N_NODES * RTILES,), 0, REMOTE // BLK), jax.random.fold_in(arg_keys[8], 1), 0, (REMOTE // BLK) - 1).astype(jnp.int32),
        "hub_tiles": draw_hub_tiles(jax.random.fold_in(arg_keys[16], 71), 0),
        "hub_dst": set_ends(jax.random.randint(arg_keys[10], (N_NODES * HTILES,), 0, NODE_DEV // BLK), jax.random.fold_in(arg_keys[10], 1), 0, (NODE_DEV // BLK) - 1).astype(jnp.int32),
        "hub_src": set_ends(jax.random.randint(arg_keys[11], (N_NODES * HTILES,), 0, HUBS // BLK), jax.random.fold_in(arg_keys[11], 1), 0, (HUBS // BLK) - 1).astype(jnp.int32),
        "self_one": noise(arg_keys[12], (F_IN, HID), F_IN ** -0.5, 0.5),
        "neigh_one": noise(arg_keys[13], (F_IN, HID), F_IN ** -0.5, 0.5),
        "self_two": noise(arg_keys[14], (HID, HID), HID ** -0.5, 0.375),
        "neigh_two": noise(arg_keys[15], (HID, HID), HID ** -0.5, 0.375),
    }


def aggregate(tiles, dst, src, source, width):
    blocks = source.reshape(-1, BLK, width)[src].astype(jnp.float32)
    prod = jnp.einsum("tij,tjf->tif", tiles.astype(jnp.float32), blocks, precision=lax.Precision.HIGHEST)
    total = jax.ops.segment_sum(prod, dst, num_segments=NODE_DEV // BLK)
    return total.reshape(NODE_DEV, width)


def row_weight(tiles, dst):
    sums = jnp.sum(tiles.astype(jnp.float32), axis=2)
    return jax.ops.segment_sum(sums, dst, num_segments=NODE_DEV // BLK).reshape(NODE_DEV)


def layer(values, send_lists, hub_rows, groups, w_self, w_neigh):
    width = values.shape[1]
    stacked = values.reshape(N_NODES, NODE_DEV, width)
    owners = jnp.arange(N_NODES, dtype=jnp.int32)
    hubs = stacked[owners[:, None], hub_rows.reshape(N_NODES, HUB_DEV)].reshape(HUBS, width)
    by_peer = jnp.transpose(send_lists, (1, 0, 2))

    def one_device(items):
        own, lists, lt, ld, ls, rt, rd, rs, ht, hd, hs = items
        remote = stacked[owners[:, None], lists].reshape(REMOTE, width)
        agg = aggregate(lt, ld, ls, own, width) + aggregate(rt, rd, rs, remote, width) + aggregate(ht, hd, hs, hubs, width)
        deg = 1.0 + row_weight(lt, ld) + row_weight(rt, rd) + row_weight(ht, hd)
        mean = (agg / deg[:, None]).astype(jnp.bfloat16)
        out = jnp.dot(own, w_self, preferred_element_type=jnp.float32) + jnp.dot(mean, w_neigh, preferred_element_type=jnp.float32)
        return jax.nn.relu(out)

    result = lax.map(one_device, (stacked, by_peer) + groups)
    return result.reshape(NODES, w_self.shape[1])


def reference(features, send_lists, hub_rows, local_tiles, local_dst, local_src, remote_tiles, remote_dst, remote_src, hub_tiles, hub_dst, hub_src, self_one, neigh_one, self_two, neigh_two):
    def split(a):
        return a.reshape((N_NODES, -1) + a.shape[1:])

    groups = tuple(split(a) for a in (local_tiles, local_dst, local_src, remote_tiles, remote_dst, remote_src, hub_tiles, hub_dst, hub_src))
    first = layer(features, send_lists, hub_rows, groups, self_one, neigh_one).astype(jnp.bfloat16)
    return layer(first, send_lists, hub_rows, groups, self_two, neigh_two)
```

```python
import functools

import jax
import jax.numpy as jnp
from jax import lax
from jax.experimental import pallas as pl
from jax.experimental.pallas import tpu as pltpu
from jax.sharding import PartitionSpec as P

F32 = jnp.float32
BF16 = jnp.bfloat16
MIB = 1024 * 1024


def params(mib):
    return pltpu.CompilerParams(vmem_limit_bytes=mib * MIB)


def whole(memory=pltpu.VMEM):
    return pl.BlockSpec(memory_space=memory)


def dot(a, b):
    return jnp.dot(a, b, preferred_element_type=F32)


def column(row, first, rows):
    shape = (rows, row.shape[1])
    sub = lax.broadcasted_iota(jnp.int32, shape, 0)
    lane = lax.broadcasted_iota(jnp.int32, shape, 1)
    picked = jnp.where(lane == sub + first, jnp.broadcast_to(row, shape), 0.0)
    return jnp.sum(picked, axis=1, keepdims=True)


def fill_send(send_rows, sel_ref, values, send_ref):
    peers = send_ref.shape[0]
    hubs = sel_ref.shape[0] - peers * send_rows
    half = hubs // 2
    rows = dot(sel_ref[...], values).astype(BF16)
    for p in range(peers):
        send_ref[p, 0:send_rows, :] = rows[p * send_rows : (p + 1) * send_rows]
        start = peers * send_rows + half * (p % 2)
        send_ref[p, send_rows : send_rows + half, :] = rows[start : start + half]


def select_kernel(x_ref, lists_ref, hub_ref, sel_ref, send_ref):
    peers, send_rows = lists_ref.shape[1:]
    nodes = x_ref.shape[0]
    hubs = hub_ref.shape[1]
    place = lax.broadcasted_iota(jnp.int32, (16, nodes), 1).astype(F32)

    def put(start, col):
        sel_ref[start : start + 16, :] = jnp.where(col == place, 1.0, 0.0).astype(BF16)

    for p in range(peers):
        row = lists_ref[0, p : p + 1, :].astype(F32)
        for c in range(0, send_rows, 16):
            put(p * send_rows + c, column(row, c, 16))
    hub_row = hub_ref[...].astype(F32)
    for c in range(0, hubs, 16):
        put(peers * send_rows + c, column(hub_row, c, 16))
    fill_send(send_rows, sel_ref, x_ref[...], send_ref)


def build_kernel(
    cols, parts, steps, ld, ls, rd, rs, hd, hs, x_ref, lt, rt, ht, al_ref, ar_ref, inv_ref, agg_ref, acc
):
    part = pl.program_id(0)
    step = pl.program_id(1)
    size = acc.shape[1]
    blocks = acc.shape[0] // sum(cols)
    wide = sum(cols)
    per = lt.shape[0]

    @pl.when(step == 0)
    def _():
        def clear(i, _):
            acc[i] = jnp.zeros((size, size), F32)
            return 0

        lax.fori_loop(0, blocks * wide, clear, 0)

    def add(i, _):
        t = step * per + i
        off = 0
        for dst, src, tiles, width in ((ld, ls, lt, cols[0]), (rd, rs, rt, cols[1]), (hd, hs, ht, cols[2])):
            d = dst[t]
            slot = d * wide + off + src[t]
            if parts > 1:
                low = part * blocks
                inside = jnp.logical_and(d >= low, d < low + blocks)
                slot = jnp.where(inside, slot - low * wide, blocks * wide)
            acc[slot] += tiles[i].astype(F32)
            off += width
        return 0

    lax.fori_loop(0, per, add, 0)

    @pl.when(step == steps - 1)
    def _():
        def finish(b, _):
            rows = pl.ds(pl.multiple_of(b * size, size), size)
            total = jnp.zeros((size, size), F32)
            for c in range(wide):
                tile = acc[b * wide + c]
                total += tile
                ref, at = (al_ref, c) if c < cols[0] else (ar_ref, c - cols[0])
                ref[rows, at * size : (at + 1) * size] = tile.astype(BF16)
            deg = 1.0 + jnp.sum(total, axis=1, keepdims=True)
            inv_ref[rows, :] = jnp.broadcast_to(1.0 / deg, (size, size))
            agg_ref[rows, :] = dot(al_ref[rows, :], x_ref[...])
            return 0

        lax.fori_loop(0, blocks, finish, 0)


def assemble(send_rows, own_ref, other_ref, dest_ref, lanes):
    peers, per = own_ref.shape[:2]
    half = per - send_rows
    mine = lax.rem(lax.axis_index("nodes"), 2)
    base = peers * send_rows
    for o in range(peers):
        dest_ref[o * send_rows : (o + 1) * send_rows, lanes] = own_ref[o, 0:send_rows, :]
        for ref, h in ((own_ref, mine), (other_ref, 1 - mine)):
            at = pl.multiple_of(base + o * 2 * half + h * half, half)
            dest_ref[pl.ds(at, half), lanes] = ref[o, send_rows:per, :]


def mean_kernel(
    send_rows, parts, own_ref, other_ref, ar_ref, agg_ref, inv_ref, sel_ref, mean_ref, send_ref, xr_ref
):
    part = pl.program_id(0)
    rows = ar_ref.shape[0]

    @pl.when(part == 0)
    def _():
        assemble(send_rows, own_ref, other_ref, xr_ref, slice(None))

    agg = agg_ref[...] + dot(ar_ref[...], xr_ref[...])
    mean_ref[pl.ds(pl.multiple_of(part * rows, rows), rows), :] = (agg * inv_ref[...]).astype(BF16)

    @pl.when(part == parts - 1)
    def _():
        fill_send(send_rows, sel_ref, mean_ref[...], send_ref)


def own_kernel(x_ref, mean_ref, al_ref, self_one, neigh_one, self_two, agg_ref, part_ref, first):
    part = pl.program_id(0)

    @pl.when(part == 0)
    def _():
        total = dot(x_ref[...], self_one[...]) + dot(mean_ref[...], neigh_one[...])
        first[...] = jnp.maximum(total, 0.0).astype(BF16)

    rows = al_ref.shape[0]
    agg_ref[...] = dot(al_ref[...], first[...])
    at = pl.ds(pl.multiple_of(part * rows, rows), rows)
    part_ref[...] = dot(first[at, :], self_two[...])


def last_kernel(
    send_rows,
    own_ref,
    other_ref,
    xr_ref,
    self_one,
    neigh_one,
    ar_ref,
    agg_ref,
    part_ref,
    inv_ref,
    neigh_two,
    out_ref,
    both,
    weight,
    first,
):
    width = xr_ref.shape[1]

    @pl.when(pl.program_id(0) == 0)
    def _():
        both[:, 0:width] = xr_ref[...]
        assemble(send_rows, own_ref, other_ref, both, slice(width, 2 * width))
        weight[0:width, :] = self_one[...]
        weight[width : 2 * width, :] = neigh_one[...]
        first[...] = jnp.maximum(dot(both[...], weight[...]), 0.0).astype(BF16)

    agg = agg_ref[...] + dot(ar_ref[...], first[...])
    inv = inv_ref[...]
    inv = jnp.concatenate([inv] * (agg.shape[1] // inv.shape[1]), axis=1)
    mean = (agg * inv).astype(BF16)
    out_ref[...] = jnp.maximum(part_ref[...] + dot(mean, neigh_two[...]), 0.0)


def per_device(
    features,
    send_lists,
    hub_rows,
    local_tiles,
    local_dst,
    local_src,
    remote_tiles,
    remote_dst,
    remote_src,
    hub_tiles,
    hub_dst,
    hub_src,
    self_one,
    neigh_one,
    self_two,
    neigh_two,
):
    nodes, f_in = features.shape
    hid = self_one.shape[1]
    tiles, size = local_tiles.shape[:2]
    _, peers, send_rows = send_lists.shape
    hubs = hub_rows.shape[0]
    per = send_rows + hubs // 2
    far = peers * (send_rows + hubs)
    cols = (nodes // size, peers * send_rows // size, peers * hubs // size)
    wide = sum(cols)
    blocks = nodes // size
    parts = 1
    while blocks * wide * size * size * 4 > parts * 16 * MIB:
        parts *= 2
    rows = nodes // parts
    spare = 0 if parts == 1 else 1
    swap = [(i, i ^ 1) for i in range(peers)]
    sds = jax.ShapeDtypeStruct
    vm = whole()

    def split(width):
        return vm if parts == 1 else pl.BlockSpec((rows, width), lambda i, *_: (i, 0))

    sel, send = pl.pallas_call(
        select_kernel,
        out_shape=(sds((peers * send_rows + hubs, nodes), BF16), sds((peers, per, f_in), BF16)),
        in_specs=[vm] * 3,
        out_specs=(vm, vm),
        compiler_params=params(32),
        name="select",
    )(features, send_lists, hub_rows.reshape(1, hubs))

    got = lax.all_to_all(send, "nodes", split_axis=0, concat_axis=0, tiled=True)

    steps = 6
    chunk = pl.BlockSpec((tiles // steps, size, size), lambda i, j, *_: (j, 0, 0))
    one = pl.Buffered(1)

    def block_out(width):
        return pl.BlockSpec((rows, width), lambda i, j, *_: (i, 0), pipeline_mode=one if parts == 1 else None)

    a_local, a_far, inv, agg = pl.pallas_call(
        functools.partial(build_kernel, cols, parts, steps),
        out_shape=(
            sds((nodes, nodes), BF16),
            sds((nodes, far), BF16),
            sds((nodes, size), F32),
            sds((nodes, f_in), F32),
        ),
        grid_spec=pltpu.PrefetchScalarGridSpec(
            num_scalar_prefetch=6,
            grid=(parts, steps),
            in_specs=[vm, chunk, chunk, chunk],
            out_specs=(block_out(nodes), block_out(far), block_out(size), block_out(f_in)),
            scratch_shapes=[pltpu.VMEM((blocks // parts * wide + spare, size, size), F32)],
        ),
        compiler_params=params(48),
        cost_estimate=pl.CostEstimate(flops=2 * nodes * nodes * f_in, bytes_accessed=40 * MIB, transcendentals=0),
        name="build",
    )(
        local_dst,
        local_src,
        remote_dst,
        remote_src,
        hub_dst,
        hub_src,
        features,
        local_tiles,
        remote_tiles,
        hub_tiles,
    )

    other = lax.ppermute(got, "nodes", swap)

    mean, send, x_far = pl.pallas_call(
        functools.partial(mean_kernel, send_rows, parts),
        out_shape=(sds((nodes, f_in), BF16), sds(send.shape, BF16), sds((far, f_in), BF16)),
        grid=(parts,),
        in_specs=[vm, vm, split(far), split(f_in), split(size), vm],
        out_specs=(vm, vm, vm),
        compiler_params=params(40),
        name="mean",
    )(got, other, a_far, agg, inv, sel)

    got = lax.all_to_all(send, "nodes", split_axis=0, concat_axis=0, tiled=True)

    agg, part = pl.pallas_call(
        own_kernel,
        out_shape=(sds((nodes, hid), F32), sds((nodes, hid), F32)),
        grid=(parts,),
        in_specs=[vm, vm, split(nodes), vm, vm, vm],
        out_specs=(split(hid), split(hid)),
        scratch_shapes=[pltpu.VMEM((nodes, hid), BF16)],
        compiler_params=params(32),
        cost_estimate=pl.CostEstimate(flops=2 * nodes * nodes * hid, bytes_accessed=20 * MIB, transcendentals=0),
        name="own",
    )(features, mean, a_local, self_one, neigh_one, self_two)

    other = lax.ppermute(got, "nodes", swap)

    return pl.pallas_call(
        functools.partial(last_kernel, send_rows),
        out_shape=sds((nodes, hid), F32),
        grid=(parts,),
        in_specs=[vm, vm, vm, vm, vm, split(far), split(hid), split(hid), split(size), vm],
        out_specs=split(hid),
        scratch_shapes=[
            pltpu.VMEM((far, 2 * f_in), BF16),
            pltpu.VMEM((2 * f_in, hid), BF16),
            pltpu.VMEM((far, hid), BF16),
        ],
        compiler_params=params(48),
        name="last",
    )(got, other, x_far, self_one, neigh_one, a_far, agg, part, inv, neigh_two)


def solution(mesh):
    placed = (
        P("nodes", None),
        P("nodes", None, None),
        P("nodes"),
        P("nodes", None, None),
        P("nodes"),
        P("nodes"),
        P("nodes", None, None),
        P("nodes"),
        P("nodes"),
        P("nodes", None, None),
        P("nodes"),
        P("nodes"),
        P(),
        P(),
        P(),
        P(),
    )
    return jax.shard_map(
        per_device, mesh=mesh, in_specs=placed, out_specs=P("nodes", None), check_vma=False
    )
```

```python
import functools

import jax
import jax.numpy as jnp
from jax import lax
from jax.experimental import pallas as pl
from jax.experimental.pallas import tpu as pltpu
from jax.sharding import PartitionSpec as P

F32 = jnp.float32
BF16 = jnp.bfloat16
MIB = 1024 * 1024


def params(mib):
    return pltpu.CompilerParams(vmem_limit_bytes=mib * MIB)


def whole(memory=pltpu.VMEM):
    return pl.BlockSpec(memory_space=memory)


def dot(a, b):
    return jnp.dot(a, b, preferred_element_type=F32)


def fill_select(lists_ref, hub_ref, sel_ref):
    send_rows, peers = lists_ref.shape
    nodes = sel_ref.shape[1]
    hubs = hub_ref.shape[1]
    place = lax.broadcasted_iota(jnp.int32, (16, nodes), 1).astype(F32)

    def put(start, col):
        sel_ref[start : start + 16, :] = jnp.where(col == place, 1.0, 0.0).astype(BF16)

    lists = lists_ref[...].astype(F32)
    for p in range(peers):
        for c in range(0, send_rows, 16):
            put(p * send_rows + c, lists[c : c + 16, p : p + 1])
    table = jnp.broadcast_to(hub_ref[...].astype(F32), (16, hubs))
    sub = lax.broadcasted_iota(jnp.int32, (16, hubs), 0)
    lane = lax.broadcasted_iota(jnp.int32, (16, hubs), 1)
    for c in range(0, hubs, 16):
        picked = jnp.where(lane == sub + c, table, 0.0)
        put(peers * send_rows + c, jnp.sum(picked, axis=1, keepdims=True))


def fill_send(send_rows, sel, values, send_ref):
    peers = send_ref.shape[0]
    half = (sel.shape[0] - peers * send_rows) // 2
    rows = dot(sel, values).astype(BF16)
    for p in range(peers):
        send_ref[p, 0:send_rows, :] = rows[p * send_rows : (p + 1) * send_rows]
        start = peers * send_rows + half * (p % 2)
        send_ref[p, send_rows : send_rows + half, :] = rows[start : start + half]


def fetch(pairs, sems):
    copies = [pltpu.make_async_copy(src, dst, sems.at[i]) for i, (src, dst) in enumerate(pairs)]
    for copy in copies:
        copy.start()
    return copies


def select_kernel(x_hbm, lists_hbm, hub_hbm, send_ref, x_ref, lists_ref, hub_ref, sel_ref, sems):
    copies = fetch(((lists_hbm, lists_ref), (hub_hbm, hub_ref), (x_hbm, x_ref)), sems)
    copies[0].wait()
    copies[1].wait()
    fill_select(lists_ref, hub_ref, sel_ref)
    copies[2].wait()
    fill_send(lists_ref.shape[0], sel_ref[...], x_ref[...], send_ref)


def build_kernel(
    cols,
    parts,
    chunks,
    ld,
    ls,
    rd,
    rs,
    hd,
    hs,
    x_hbm,
    lt,
    rt,
    ht,
    al_ref,
    ar_hbm,
    inv_hbm,
    agg_ref,
    acc,
    tiles,
    x_ref,
    ar_ref,
    inv_ref,
    tile_sems,
    x_sem,
    out_sems,
):
    part = pl.program_id(0)
    size = acc.shape[1]
    wide = sum(cols)
    blocks = acc.shape[0] // wide
    count = lt.shape[0]
    per = count // chunks
    index = ((ld, ls), (rd, rs), (hd, hs))
    groups = (lt, rt, ht)
    moves = [
        [
            pltpu.make_async_copy(
                groups[g].at[pl.ds(k * per, per)], tiles.at[g, pl.ds(k * per, per)], tile_sems.at[g, k]
            )
            for k in range(chunks)
        ]
        for g in range(3)
    ]
    load_x = pltpu.make_async_copy(x_hbm, x_ref, x_sem)

    @pl.when(part == 0)
    def _():
        for g in range(3):
            for k in range(chunks):
                moves[g][k].start()
        load_x.start()

    def clear(i, _):
        acc[i] = jnp.zeros((size, size), F32)
        return 0

    lax.fori_loop(0, acc.shape[0], clear, 0, unroll=4)

    off = 0
    for g in range(3):
        for k in range(chunks):

            @pl.when(part == 0)
            def _(move=moves[g][k]):
                move.wait()

            def add(i, _, g=g, k=k, off=off):
                t = k * per + i
                d = index[g][0][t]
                slot = d * wide + off + index[g][1][t]
                if parts > 1:
                    low = part * blocks
                    inside = jnp.logical_and(d >= low, d < low + blocks)
                    slot = jnp.where(inside, slot - low * wide, blocks * wide)
                acc[slot] += tiles[g, t].astype(F32)
                return 0

            lax.fori_loop(0, per, add, 0, unroll=4)
        off += cols[g]

    @pl.when(part == 0)
    def _():
        load_x.wait()

    def leave(b):
        rows = pl.ds(pl.multiple_of(b * size, size), size)
        there = pl.ds(pl.multiple_of((part * blocks + b) * size, size), size)
        return (
            pltpu.make_async_copy(ar_ref.at[rows], ar_hbm.at[there], out_sems.at[0, b]),
            pltpu.make_async_copy(inv_ref.at[rows], inv_hbm.at[there], out_sems.at[1, b]),
        )

    def finish(b, _):
        rows = pl.ds(pl.multiple_of(b * size, size), size)
        total = jnp.zeros((size, size), F32)
        for c in range(wide):
            tile = acc[b * wide + c]
            total += tile
            ref, at = (al_ref, c) if c < cols[0] else (ar_ref, c - cols[0])
            ref[rows, at * size : (at + 1) * size] = tile.astype(BF16)
        deg = 1.0 + jnp.sum(total, axis=1, keepdims=True)
        inv_ref[rows, :] = jnp.broadcast_to(1.0 / deg, (size, size))
        for copy in leave(b):
            copy.start()
        agg_ref[rows, :] = dot(al_ref[rows, :], x_ref[...])
        return 0

    lax.fori_loop(0, blocks, finish, 0)

    def end(b, _):
        for copy in leave(b):
            copy.wait()
        return 0

    lax.fori_loop(0, blocks, end, 0)


def assemble(send_rows, own_ref, other_ref, dest_ref, lanes):
    peers, per = own_ref.shape[:2]
    half = per - send_rows
    mine = lax.rem(lax.axis_index("nodes"), 2)
    base = peers * send_rows
    for o in range(peers):
        dest_ref[o * send_rows : (o + 1) * send_rows, lanes] = own_ref[o, 0:send_rows, :]
        for ref, h in ((own_ref, mine), (other_ref, 1 - mine)):
            at = pl.multiple_of(base + o * 2 * half + h * half, half)
            dest_ref[pl.ds(at, half), lanes] = ref[o, send_rows:per, :]


def stage_kernel(lists_hbm, hub_hbm, _, *refs):
    pairs = len(refs) // 2 - 2
    sources, targets = refs[:pairs], refs[pairs : 2 * pairs]
    sel_ref, lists_ref, hub_ref, sems = refs[2 * pairs :]
    copies = fetch(((lists_hbm, lists_ref), (hub_hbm, hub_ref), *zip(sources, targets)), sems)
    copies[0].wait()
    copies[1].wait()
    fill_select(lists_ref, hub_ref, sel_ref)
    for copy in copies[2:]:
        copy.wait()


def cuts_of(rows, cuts):
    return [slice(k * rows // cuts, (k + 1) * rows // cuts) for k in range(cuts)]


def mean_kernel(
    send_rows, parts, own_ref, other_ref, agg_ref, a_ref, inv_ref, sel_ref, mean_ref, send_ref, xr_ref
):
    part = pl.program_id(0)
    rows = a_ref.shape[0]

    @pl.when(part == 0)
    def _():
        assemble(send_rows, own_ref, other_ref, xr_ref, slice(None))

    for at in cuts_of(rows, 4):
        agg = agg_ref[at, :] + dot(a_ref[at, :], xr_ref[...])
        there = pl.ds(pl.multiple_of(part * rows + at.start, rows // 4), rows // 4)
        mean_ref[there, :] = (agg * inv_ref[at, :]).astype(BF16)

    @pl.when(part == parts - 1)
    def _():
        fill_send(send_rows, sel_ref[...], mean_ref[...], send_ref)


def own_kernel(x_ref, mean_ref, a_ref, self_one, neigh_one, self_two, agg_ref, part_ref, first):
    part = pl.program_id(0)
    rows = a_ref.shape[0]

    @pl.when(part == 0)
    def _():
        total = dot(x_ref[...], self_one[...]) + dot(mean_ref[...], neigh_one[...])
        first[...] = jnp.maximum(total, 0.0).astype(BF16)

    for at in cuts_of(rows, 4):
        agg_ref[at, :] = dot(a_ref[at, :], first[...])
    at = pl.ds(pl.multiple_of(part * rows, rows), rows)
    part_ref[...] = dot(first[at, :], self_two[...])


def last_kernel(
    send_rows,
    own_one,
    other_one,
    own_two,
    other_two,
    agg_ref,
    part_ref,
    inv_ref,
    a_ref,
    self_one,
    neigh_one,
    neigh_two,
    out_hbm,
    both,
    weight,
    first,
    out_ref,
    sems,
):
    part = pl.program_id(0)
    rows = a_ref.shape[0]
    width = both.shape[1] // 2

    @pl.when(part == 0)
    def _():
        assemble(send_rows, own_one, other_one, both, slice(0, width))
        assemble(send_rows, own_two, other_two, both, slice(width, 2 * width))
        weight[0:width, :] = self_one[...]
        weight[width : 2 * width, :] = neigh_one[...]
        first[...] = jnp.maximum(dot(both[...], weight[...]), 0.0).astype(BF16)

    outs = []
    for k, at in enumerate(cuts_of(rows, 4)):
        agg = agg_ref[at, :] + dot(a_ref[at, :], first[...])
        inv = inv_ref[at, :]
        inv = jnp.concatenate([inv] * (agg.shape[1] // inv.shape[1]), axis=1)
        mean = (agg * inv).astype(BF16)
        out_ref[at, :] = jnp.maximum(part_ref[at, :] + dot(mean, neigh_two[...]), 0.0)
        there = pl.ds(pl.multiple_of(part * rows + at.start, rows // 4), rows // 4)
        outs.append(pltpu.make_async_copy(out_ref.at[at], out_hbm.at[there], sems.at[k]))
        outs[k].start()
    for copy in outs:
        copy.wait()


def per_device(
    features,
    send_lists,
    hub_rows,
    local_tiles,
    local_dst,
    local_src,
    remote_tiles,
    remote_dst,
    remote_src,
    hub_tiles,
    hub_dst,
    hub_src,
    self_one,
    neigh_one,
    self_two,
    neigh_two,
):
    nodes, f_in = features.shape
    hid = self_one.shape[1]
    tiles, size = local_tiles.shape[:2]
    _, peers, send_rows = send_lists.shape
    hubs = hub_rows.shape[0]
    per = send_rows + hubs // 2
    far = peers * (send_rows + hubs)
    cols = (nodes // size, peers * send_rows // size, peers * hubs // size)
    wide = sum(cols)
    blocks = nodes // size
    parts = 1
    while blocks * wide * size * size * 4 > parts * 16 * MIB:
        parts *= 2
    rows = nodes // parts
    spare = 0 if parts == 1 else 1
    swap = [(i, i ^ 1) for i in range(peers)]
    sds = jax.ShapeDtypeStruct
    vm = whole()
    hbm = whole(pltpu.HBM)

    def split(width):
        return vm if parts == 1 else pl.BlockSpec((rows, width), lambda i, *_: (i, 0))

    dma = pltpu.SemaphoreType.DMA

    def in_hbm(*arrays):
        return [pltpu.with_memory_space_constraint(a, pltpu.HBM) for a in arrays]

    def kept(shape, dtype):
        return sds(shape, dtype) if parts > 1 else pltpu.VMEM(shape, dtype)

    lists = send_lists[0].T
    hub_row = hub_rows.reshape(1, hubs)
    chosen = peers * send_rows + hubs
    tables = [pltpu.VMEM((send_rows, peers), jnp.int32), pltpu.VMEM((1, hubs), jnp.int32)]
    send = pl.pallas_call(
        select_kernel,
        out_shape=kept((peers, per, f_in), BF16),
        in_specs=[hbm] * 3,
        out_specs=vm,
        scratch_shapes=[pltpu.VMEM((nodes, f_in), BF16), *tables, pltpu.VMEM((chosen, nodes), BF16), dma((3,))],
        compiler_params=params(16),
        name="select",
    )(*in_hbm(features, lists, hub_row))

    got = lax.all_to_all(send, "nodes", split_axis=0, concat_axis=0, tiled=True)

    chunks = 2
    a_local, a_far, inv, agg = pl.pallas_call(
        functools.partial(build_kernel, cols, parts, chunks),
        out_shape=(
            kept((nodes, nodes), BF16),
            pltpu.HBM((nodes, far), BF16),
            pltpu.HBM((nodes, size), F32),
            kept((nodes, f_in), F32),
        ),
        grid=(parts,),
        in_specs=[whole(pltpu.SMEM)] * 6 + [hbm] * 4,
        out_specs=(split(nodes), hbm, hbm, split(f_in)),
        scratch_shapes=[
            pltpu.VMEM((blocks // parts * wide + spare, size, size), F32),
            pltpu.VMEM((3, tiles, size, size), BF16),
            pltpu.VMEM((nodes, f_in), BF16),
            pltpu.VMEM((rows, far), BF16),
            pltpu.VMEM((rows, size), F32),
            dma((3, chunks)),
            dma(()),
            dma((2, blocks // parts)),
        ],
        compiler_params=params(36 if parts == 1 else 48),
        cost_estimate=pl.CostEstimate(flops=2 * nodes * nodes * f_in, bytes_accessed=40 * MIB, transcendentals=0),
        name="build",
    )(
        *in_hbm(local_dst, local_src, remote_dst, remote_src, hub_dst, hub_src),
        *in_hbm(features, local_tiles, remote_tiles, hub_tiles),
    )
    got, a_local, a_far, inv, agg = lax.optimization_barrier((got, a_local, a_far, inv, agg))

    other = lax.ppermute(got, "nodes", swap)

    staged = (a_far, inv) if parts == 1 else ()
    *moved, sel = pl.pallas_call(
        stage_kernel,
        out_shape=(*(kept(x.shape, x.dtype) for x in staged), kept((chosen, nodes), BF16)),
        in_specs=[hbm, hbm, whole(pl.ANY)] + [hbm] * len(staged),
        out_specs=(vm,) * (1 + len(staged)),
        scratch_shapes=[*tables, dma((2 + len(staged),))],
        compiler_params=params(8 if parts == 1 else 16),
        cost_estimate=pl.CostEstimate(flops=0, bytes_accessed=8 * MIB, transcendentals=0),
        name="stage",
    )(*in_hbm(lists, hub_row), got, *in_hbm(*staged))
    if staged:
        a_far, inv = moved

    mean, send = pl.pallas_call(
        functools.partial(mean_kernel, send_rows, parts),
        out_shape=(sds((nodes, f_in), BF16), sds(send.shape, BF16)),
        grid=(parts,),
        in_specs=[vm] * 2 + [split(f_in), split(far), split(size), vm],
        out_specs=(vm, vm),
        scratch_shapes=[pltpu.VMEM((far, f_in), BF16)],
        compiler_params=params(8 if parts == 1 else 48),
        name="mean",
    )(got, other, agg, a_far, inv, sel)

    got_two = lax.all_to_all(send, "nodes", split_axis=0, concat_axis=0, tiled=True)
    got_two, mean = lax.optimization_barrier((got_two, mean))
    other_two = lax.ppermute(got_two, "nodes", swap)

    agg, part = pl.pallas_call(
        own_kernel,
        out_shape=(sds((nodes, hid), F32), sds((nodes, hid), F32)),
        grid=(parts,),
        in_specs=[vm, vm, split(nodes), vm, vm, vm],
        out_specs=(split(hid), split(hid)),
        scratch_shapes=[pltpu.VMEM((nodes, hid), BF16)],
        compiler_params=params(16),
        cost_estimate=pl.CostEstimate(flops=2 * nodes * nodes * hid, bytes_accessed=8 * MIB, transcendentals=0),
        name="own",
    )(features, mean, a_local, self_one, neigh_one, self_two)

    return pl.pallas_call(
        functools.partial(last_kernel, send_rows),
        out_shape=sds((nodes, hid), F32),
        grid=(parts,),
        in_specs=[vm] * 4 + [split(hid), split(hid), split(size), split(far)] + [vm] * 3,
        out_specs=hbm,
        scratch_shapes=[
            pltpu.VMEM((far, 2 * f_in), BF16),
            pltpu.VMEM((2 * f_in, hid), BF16),
            pltpu.VMEM((far, hid), BF16),
            pltpu.VMEM((rows, hid), F32),
            dma((4,)),
        ],
        compiler_params=params(16 if parts == 1 else 56),
        name="last",
    )(got, other, got_two, other_two, agg, part, inv, a_far, self_one, neigh_one, neigh_two)


def solution(mesh):
    placed = (
        P("nodes", None),
        P("nodes", None, None),
        P("nodes"),
        P("nodes", None, None),
        P("nodes"),
        P("nodes"),
        P("nodes", None, None),
        P("nodes"),
        P("nodes"),
        P("nodes", None, None),
        P("nodes"),
        P("nodes"),
        P(),
        P(),
        P(),
        P(),
    )
    return jax.shard_map(
        per_device, mesh=mesh, in_specs=placed, out_specs=P("nodes", None), check_vma=False
    )
```

```python
import functools

import jax
import jax.numpy as jnp
from jax import lax
from jax.experimental import pallas as pl
from jax.experimental.pallas import tpu as pltpu
from jax.sharding import PartitionSpec as P

F32 = jnp.float32
BF16 = jnp.bfloat16
MIB = 1024 * 1024


def params(mib):
    return pltpu.CompilerParams(vmem_limit_bytes=mib * MIB)


def whole(memory=pltpu.VMEM):
    return pl.BlockSpec(memory_space=memory)


def dot(a, b):
    return jnp.dot(a, b, preferred_element_type=F32)


def fill_select(lists_ref, hub_ref, sel_ref):
    send_rows, peers = lists_ref.shape
    nodes = sel_ref.shape[1]
    hubs = hub_ref.shape[1]
    place = lax.broadcasted_iota(jnp.int32, (16, nodes), 1).astype(F32)

    def put(start, col):
        sel_ref[start : start + 16, :] = jnp.where(col == place, 1.0, 0.0).astype(BF16)

    lists = lists_ref[...].astype(F32)
    for p in range(peers):
        for c in range(0, send_rows, 16):
            put(p * send_rows + c, lists[c : c + 16, p : p + 1])
    table = jnp.broadcast_to(hub_ref[...].astype(F32), (16, hubs))
    sub = lax.broadcasted_iota(jnp.int32, (16, hubs), 0)
    lane = lax.broadcasted_iota(jnp.int32, (16, hubs), 1)
    for c in range(0, hubs, 16):
        picked = jnp.where(lane == sub + c, table, 0.0)
        put(peers * send_rows + c, jnp.sum(picked, axis=1, keepdims=True))


def fill_send(send_rows, sel, values, send_ref):
    peers = send_ref.shape[0]
    half = (sel.shape[0] - peers * send_rows) // 2
    rows = dot(sel, values).astype(BF16)
    for p in range(peers):
        send_ref[p, 0:send_rows, :] = rows[p * send_rows : (p + 1) * send_rows]
        start = peers * send_rows + half * (p % 2)
        send_ref[p, send_rows : send_rows + half, :] = rows[start : start + half]


def fetch(pairs, sems):
    copies = [pltpu.make_async_copy(src, dst, sems.at[i]) for i, (src, dst) in enumerate(pairs)]
    for copy in copies:
        copy.start()
    return copies


def select_kernel(x_hbm, lists_hbm, hub_hbm, send_ref, x_ref, lists_ref, hub_ref, sel_ref, sems):
    copies = fetch(((lists_hbm, lists_ref), (hub_hbm, hub_ref), (x_hbm, x_ref)), sems)
    copies[0].wait()
    copies[1].wait()
    fill_select(lists_ref, hub_ref, sel_ref)
    copies[2].wait()
    fill_send(lists_ref.shape[0], sel_ref[...], x_ref[...], send_ref)


def build_kernel(
    cols,
    parts,
    chunks,
    ld,
    ls,
    rd,
    rs,
    hd,
    hs,
    x_hbm,
    lt,
    rt,
    ht,
    al_hbm,
    ar_hbm,
    inv_hbm,
    near_ref,
    agg_ref,
    acc,
    tiles,
    x_ref,
    al_ref,
    ar_ref,
    inv_ref,
    tile_sems,
    x_sem,
    out_sems,
):
    part = pl.program_id(0)
    size = acc.shape[1]
    wide = sum(cols)
    near = wide - near_ref.shape[1] // size
    blocks = acc.shape[0] // wide
    count = lt.shape[0]
    per = count // chunks
    index = ((ld, ls), (rd, rs), (hd, hs))
    groups = (lt, rt, ht)
    moves = [
        [
            pltpu.make_async_copy(
                groups[g].at[pl.ds(k * per, per)], tiles.at[g, pl.ds(k * per, per)], tile_sems.at[g, k]
            )
            for k in range(chunks)
        ]
        for g in range(3)
    ]
    load_x = pltpu.make_async_copy(x_hbm, x_ref, x_sem)

    @pl.when(part == 0)
    def _():
        for g in range(3):
            for k in range(chunks):
                moves[g][k].start()
        load_x.start()

    def clear(i, _):
        acc[i] = jnp.zeros((size, size), F32)
        return 0

    lax.fori_loop(0, acc.shape[0], clear, 0, unroll=4)

    off = 0
    for g in range(3):
        for k in range(chunks):

            @pl.when(part == 0)
            def _(move=moves[g][k]):
                move.wait()

            def add(i, _, g=g, k=k, off=off):
                t = k * per + i
                d = index[g][0][t]
                slot = d * wide + off + index[g][1][t]
                if parts > 1:
                    low = part * blocks
                    inside = jnp.logical_and(d >= low, d < low + blocks)
                    slot = jnp.where(inside, slot - low * wide, blocks * wide)
                acc[slot] += tiles[g, t].astype(F32)
                return 0

            lax.fori_loop(0, per, add, 0, unroll=4)
        off += cols[g]

    @pl.when(part == 0)
    def _():
        load_x.wait()

    def leave(b):
        rows = pl.ds(pl.multiple_of(b * size, size), size)
        there = pl.ds(pl.multiple_of((part * blocks + b) * size, size), size)
        return (
            pltpu.make_async_copy(ar_ref.at[rows], ar_hbm.at[there], out_sems.at[0, b]),
            pltpu.make_async_copy(inv_ref.at[rows], inv_hbm.at[there], out_sems.at[1, b]),
            pltpu.make_async_copy(al_ref.at[rows], al_hbm.at[there], out_sems.at[2, b]),
        )

    def finish(b, _):
        rows = pl.ds(pl.multiple_of(b * size, size), size)
        total = jnp.zeros((size, size), F32)
        for c in range(wide):
            tile = acc[b * wide + c]
            total += tile
            if c < cols[0]:
                ref, at = al_ref, c
            elif c < near:
                ref, at = ar_ref, c - cols[0]
            else:
                ref, at = near_ref, c - near
            ref[rows, at * size : (at + 1) * size] = tile.astype(BF16)
        deg = 1.0 + jnp.sum(total, axis=1, keepdims=True)
        inv_ref[rows, :] = jnp.broadcast_to(1.0 / deg, (size, size))
        for copy in leave(b):
            copy.start()
        agg_ref[rows, :] = dot(al_ref[rows, :], x_ref[...])
        return 0

    lax.fori_loop(0, blocks, finish, 0)

    def end(b, _):
        for copy in leave(b):
            copy.wait()
        return 0

    lax.fori_loop(0, blocks, end, 0)


def assemble(send_rows, own_ref, other_ref, dest_ref, lanes):
    peers, per = own_ref.shape[:2]
    half = per - send_rows
    mine = lax.rem(lax.axis_index("nodes"), 2)
    base = peers * send_rows
    for o in range(peers):
        dest_ref[o * send_rows : (o + 1) * send_rows, lanes] = own_ref[o, 0:send_rows, :]
        for ref, h in ((own_ref, mine), (other_ref, 1 - mine)):
            at = pl.multiple_of(base + o * 2 * half + h * half, half)
            dest_ref[pl.ds(at, half), lanes] = ref[o, send_rows:per, :]


def stage_kernel(lists_hbm, hub_hbm, _, *refs):
    pairs = len(refs) // 2 - 2
    sources, targets = refs[:pairs], refs[pairs : 2 * pairs]
    sel_ref, lists_ref, hub_ref, sems = refs[2 * pairs :]
    copies = fetch(((lists_hbm, lists_ref), (hub_hbm, hub_ref), *zip(sources, targets)), sems)
    copies[0].wait()
    copies[1].wait()
    fill_select(lists_ref, hub_ref, sel_ref)
    for copy in copies[2:]:
        copy.wait()


def far_dot(a_ref, near_ref, at, values_ref):
    split = a_ref.shape[1]
    return dot(a_ref[at, :], values_ref[0:split, :]) + dot(near_ref[at, :], values_ref[split:, :])


def cuts_of(rows, cuts):
    return [slice(k * rows // cuts, (k + 1) * rows // cuts) for k in range(cuts)]


def mean_kernel(
    send_rows, parts, own_ref, other_ref, agg_ref, a_ref, near_ref, inv_ref, sel_ref, mean_ref, send_ref, xr_ref
):
    part = pl.program_id(0)
    rows = a_ref.shape[0]

    @pl.when(part == 0)
    def _():
        assemble(send_rows, own_ref, other_ref, xr_ref, slice(None))

    for at in cuts_of(rows, 4):
        agg = agg_ref[at, :] + far_dot(a_ref, near_ref, at, xr_ref)
        there = pl.ds(pl.multiple_of(part * rows + at.start, rows // 4), rows // 4)
        mean_ref[there, :] = (agg * inv_ref[at, :]).astype(BF16)

    @pl.when(part == parts - 1)
    def _():
        fill_send(send_rows, sel_ref[...], mean_ref[...], send_ref)


def own_kernel(x_ref, mean_ref, a_ref, self_one, neigh_one, self_two, agg_ref, part_ref, first):
    part = pl.program_id(0)
    rows = a_ref.shape[0]

    @pl.when(part == 0)
    def _():
        total = dot(x_ref[...], self_one[...]) + dot(mean_ref[...], neigh_one[...])
        first[...] = jnp.maximum(total, 0.0).astype(BF16)

    for at in cuts_of(rows, 4):
        agg_ref[at, :] = dot(a_ref[at, :], first[...])
    at = pl.ds(pl.multiple_of(part * rows, rows), rows)
    part_ref[...] = dot(first[at, :], self_two[...])


def last_kernel(
    send_rows,
    own_one,
    other_one,
    own_two,
    other_two,
    agg_ref,
    part_ref,
    inv_ref,
    a_ref,
    near_ref,
    self_one,
    neigh_one,
    neigh_two,
    out_hbm,
    both,
    weight,
    first,
    mean_ref,
    out_ref,
    sems,
):
    part = pl.program_id(0)
    rows = a_ref.shape[0]
    width = both.shape[1] // 2

    @pl.when(part == 0)
    def _():
        assemble(send_rows, own_one, other_one, both, slice(0, width))
        assemble(send_rows, own_two, other_two, both, slice(width, 2 * width))
        weight[0:width, :] = self_one[...]
        weight[width : 2 * width, :] = neigh_one[...]
        first[...] = jnp.maximum(dot(both[...], weight[...]), 0.0).astype(BF16)

    for at in cuts_of(rows, 4):
        agg = agg_ref[at, :] + far_dot(a_ref, near_ref, at, first)
        inv = inv_ref[at, :]
        inv = jnp.concatenate([inv] * (agg.shape[1] // inv.shape[1]), axis=1)
        mean_ref[at, :] = (agg * inv).astype(BF16)
    outs = []
    for k, at in enumerate(cuts_of(rows, 4)):
        out_ref[at, :] = jnp.maximum(part_ref[at, :] + dot(mean_ref[at, :], neigh_two[...]), 0.0)
        there = pl.ds(pl.multiple_of(part * rows + at.start, rows // 4), rows // 4)
        outs.append(pltpu.make_async_copy(out_ref.at[at], out_hbm.at[there], sems.at[k]))
        outs[k].start()
    for copy in outs:
        copy.wait()


def per_device(
    features,
    send_lists,
    hub_rows,
    local_tiles,
    local_dst,
    local_src,
    remote_tiles,
    remote_dst,
    remote_src,
    hub_tiles,
    hub_dst,
    hub_src,
    self_one,
    neigh_one,
    self_two,
    neigh_two,
):
    nodes, f_in = features.shape
    hid = self_one.shape[1]
    tiles, size = local_tiles.shape[:2]
    _, peers, send_rows = send_lists.shape
    hubs = hub_rows.shape[0]
    per = send_rows + hubs // 2
    far = peers * (send_rows + hubs)
    cols = (nodes // size, peers * send_rows // size, peers * hubs // size)
    wide = sum(cols)
    blocks = nodes // size
    parts = 1
    while blocks * wide * size * size * 4 > parts * 16 * MIB:
        parts *= 2
    rows = nodes // parts
    spare = 0 if parts == 1 else 1
    swap = [(i, i ^ 1) for i in range(peers)]
    sds = jax.ShapeDtypeStruct
    vm = whole()
    hbm = whole(pltpu.HBM)

    def split(width):
        return vm if parts == 1 else pl.BlockSpec((rows, width), lambda i, *_: (i, 0))

    dma = pltpu.SemaphoreType.DMA

    def in_hbm(*arrays):
        return [pltpu.with_memory_space_constraint(a, pltpu.HBM) for a in arrays]

    def kept(shape, dtype):
        return sds(shape, dtype) if parts > 1 else pltpu.VMEM(shape, dtype)

    lists = send_lists[0].T
    hub_row = hub_rows.reshape(1, hubs)
    chosen = peers * send_rows + hubs
    tables = [pltpu.VMEM((send_rows, peers), jnp.int32), pltpu.VMEM((1, hubs), jnp.int32)]
    send = pl.pallas_call(
        select_kernel,
        out_shape=kept((peers, per, f_in), BF16),
        in_specs=[hbm] * 3,
        out_specs=vm,
        scratch_shapes=[pltpu.VMEM((nodes, f_in), BF16), *tables, pltpu.VMEM((chosen, nodes), BF16), dma((3,))],
        compiler_params=params(16),
        name="select",
    )(*in_hbm(features, lists, hub_row))

    got = lax.all_to_all(send, "nodes", split_axis=0, concat_axis=0, tiled=True)

    chunks = 2
    near = nodes
    a_local, a_far, inv, a_near, agg = pl.pallas_call(
        functools.partial(build_kernel, cols, parts, chunks),
        out_shape=(
            pltpu.HBM((nodes, nodes), BF16),
            pltpu.HBM((nodes, far - near), BF16),
            pltpu.HBM((nodes, size), F32),
            kept((nodes, near), BF16),
            kept((nodes, f_in), F32),
        ),
        grid=(parts,),
        in_specs=[whole(pltpu.SMEM)] * 6 + [hbm] * 4,
        out_specs=(hbm, hbm, hbm, split(near), split(f_in)),
        scratch_shapes=[
            pltpu.VMEM((blocks // parts * wide + spare, size, size), F32),
            pltpu.VMEM((3, tiles, size, size), BF16),
            pltpu.VMEM((nodes, f_in), BF16),
            pltpu.VMEM((rows, nodes), BF16),
            pltpu.VMEM((rows, far - near), BF16),
            pltpu.VMEM((rows, size), F32),
            dma((3, chunks)),
            dma(()),
            dma((3, blocks // parts)),
        ],
        compiler_params=params(36 if parts == 1 else 48),
        cost_estimate=pl.CostEstimate(flops=2 * nodes * nodes * f_in, bytes_accessed=40 * MIB, transcendentals=0),
        name="build",
    )(
        *in_hbm(local_dst, local_src, remote_dst, remote_src, hub_dst, hub_src),
        *in_hbm(features, local_tiles, remote_tiles, hub_tiles),
    )
    built = (got, a_local, a_far, inv, a_near, agg)
    got, a_local, a_far, inv, a_near, agg = lax.optimization_barrier(built)

    other = lax.ppermute(got, "nodes", swap)

    staged = (a_far, inv) if parts == 1 else ()
    *moved, sel = pl.pallas_call(
        stage_kernel,
        out_shape=(*(kept(x.shape, x.dtype) for x in staged), kept((chosen, nodes), BF16)),
        in_specs=[hbm, hbm, whole(pl.ANY)] + [hbm] * len(staged),
        out_specs=(vm,) * (1 + len(staged)),
        scratch_shapes=[*tables, dma((2 + len(staged),))],
        compiler_params=params(8 if parts == 1 else 16),
        cost_estimate=pl.CostEstimate(flops=0, bytes_accessed=8 * MIB, transcendentals=0),
        name="stage",
    )(*in_hbm(lists, hub_row), got, *in_hbm(*staged))
    if staged:
        a_far, inv = moved

    mean, send = pl.pallas_call(
        functools.partial(mean_kernel, send_rows, parts),
        out_shape=(sds((nodes, f_in), BF16), sds(send.shape, BF16)),
        grid=(parts,),
        in_specs=[vm] * 2 + [split(f_in), split(far - near), split(near), split(size), vm],
        out_specs=(vm, vm),
        scratch_shapes=[pltpu.VMEM((far, f_in), BF16)],
        compiler_params=params(8 if parts == 1 else 48),
        name="mean",
    )(got, other, agg, a_far, a_near, inv, sel)

    got_two = lax.all_to_all(send, "nodes", split_axis=0, concat_axis=0, tiled=True)
    got_two, mean = lax.optimization_barrier((got_two, mean))
    other_two = lax.ppermute(got_two, "nodes", swap)

    agg, part = pl.pallas_call(
        own_kernel,
        out_shape=(sds((nodes, hid), F32), sds((nodes, hid), F32)),
        grid=(parts,),
        in_specs=[vm, vm, split(nodes), vm, vm, vm],
        out_specs=(split(hid), split(hid)),
        scratch_shapes=[pltpu.VMEM((nodes, hid), BF16)],
        compiler_params=params(16),
        cost_estimate=pl.CostEstimate(flops=2 * nodes * nodes * hid, bytes_accessed=8 * MIB, transcendentals=0),
        name="own",
    )(features, mean, a_local, self_one, neigh_one, self_two)

    return pl.pallas_call(
        functools.partial(last_kernel, send_rows),
        out_shape=sds((nodes, hid), F32),
        grid=(parts,),
        in_specs=[vm] * 4 + [split(hid), split(hid), split(size), split(far - near), split(near)] + [vm] * 3,
        out_specs=hbm,
        scratch_shapes=[
            pltpu.VMEM((far, 2 * f_in), BF16),
            pltpu.VMEM((2 * f_in, hid), BF16),
            pltpu.VMEM((far, hid), BF16),
            pltpu.VMEM((rows, hid), BF16),
            pltpu.VMEM((rows, hid), F32),
            dma((4,)),
        ],
        compiler_params=params(16 if parts == 1 else 56),
        name="last",
    )(got, other, got_two, other_two, agg, part, inv, a_far, a_near, self_one, neigh_one, neigh_two)


def solution(mesh):
    placed = (
        P("nodes", None),
        P("nodes", None, None),
        P("nodes"),
        P("nodes", None, None),
        P("nodes"),
        P("nodes"),
        P("nodes", None, None),
        P("nodes"),
        P("nodes"),
        P("nodes", None, None),
        P("nodes"),
        P("nodes"),
        P(),
        P(),
        P(),
        P(),
    )
    return jax.shard_map(
        per_device, mesh=mesh, in_specs=placed, out_specs=P("nodes", None), check_vma=False
    )
```

```python
import functools

import jax
import jax.numpy as jnp
from jax import lax
from jax.experimental import pallas as pl
from jax.experimental.pallas import tpu as pltpu
from jax.sharding import PartitionSpec as P

F32 = jnp.float32
BF16 = jnp.bfloat16
MIB = 1024 * 1024


def params(mib):
    return pltpu.CompilerParams(vmem_limit_bytes=mib * MIB)


def whole(memory=pltpu.VMEM):
    return pl.BlockSpec(memory_space=memory)


def dot(a, b):
    return jnp.dot(a, b, preferred_element_type=F32)


def fill_select(lists_ref, hub_ref, sel_ref):
    send_rows, peers = lists_ref.shape
    nodes = sel_ref.shape[1]
    hubs = hub_ref.shape[1]
    place = lax.broadcasted_iota(jnp.int32, (16, nodes), 1).astype(F32)

    def put(start, col):
        sel_ref[start : start + 16, :] = jnp.where(col == place, 1.0, 0.0).astype(BF16)

    lists = lists_ref[...].astype(F32)
    for p in range(peers):
        for c in range(0, send_rows, 16):
            put(p * send_rows + c, lists[c : c + 16, p : p + 1])
    table = jnp.broadcast_to(hub_ref[...].astype(F32), (16, hubs))
    sub = lax.broadcasted_iota(jnp.int32, (16, hubs), 0)
    lane = lax.broadcasted_iota(jnp.int32, (16, hubs), 1)
    for c in range(0, hubs, 16):
        picked = jnp.where(lane == sub + c, table, 0.0)
        put(peers * send_rows + c, jnp.sum(picked, axis=1, keepdims=True))


def fill_send(send_rows, sel, values, send_ref):
    peers = send_ref.shape[0]
    half = (sel.shape[0] - peers * send_rows) // 2
    rows = dot(sel, values).astype(BF16)
    for p in range(peers):
        send_ref[p, 0:send_rows, :] = rows[p * send_rows : (p + 1) * send_rows]
        start = peers * send_rows + half * (p % 2)
        send_ref[p, send_rows : send_rows + half, :] = rows[start : start + half]


def fetch(pairs, sems):
    copies = [pltpu.make_async_copy(src, dst, sems.at[i]) for i, (src, dst) in enumerate(pairs)]
    for copy in copies:
        copy.start()
    return copies


def select_kernel(x_hbm, lists_hbm, hub_hbm, send_ref, x_ref, lists_ref, hub_ref, sel_ref, sems):
    copies = fetch(((lists_hbm, lists_ref), (hub_hbm, hub_ref), (x_hbm, x_ref)), sems)
    copies[0].wait()
    copies[1].wait()
    fill_select(lists_ref, hub_ref, sel_ref)
    copies[2].wait()
    fill_send(lists_ref.shape[0], sel_ref[...], x_ref[...], send_ref)


def halves_matrix(size, hubs):
    half = hubs // 2
    shape = (2 * size, 2 * size)
    source = lax.broadcasted_iota(jnp.int32, shape, 0)
    target = lax.broadcasted_iota(jnp.int32, shape, 1)
    mine = lax.rem(lax.axis_index("nodes"), 2)
    inner = lax.rem(target, size)
    which = jnp.where(target < size, mine, 1 - mine)
    wanted = lax.div(inner, half) * hubs + which * half + lax.rem(inner, half)
    return jnp.where(source == wanted, 1.0, 0.0).astype(BF16)


def build_kernel(
    cols,
    hubs,
    parts,
    chunks,
    ld,
    ls,
    rd,
    rs,
    hd,
    hs,
    x_hbm,
    lt,
    rt,
    ht,
    al_hbm,
    bound_hbm,
    other_hbm,
    own_ref,
    inv_ref,
    agg_ref,
    acc,
    tiles,
    x_ref,
    move,
    al_ref,
    bound_ref,
    other_ref,
    tile_sems,
    x_sem,
    out_sems,
):
    part = pl.program_id(0)
    size = acc.shape[1]
    wide = sum(cols)
    near = cols[0] + cols[1]
    blocks = acc.shape[0] // wide
    count = lt.shape[0]
    per = count // chunks
    index = ((ld, ls), (rd, rs), (hd, hs))
    groups = (lt, rt, ht)
    moves = [
        [
            pltpu.make_async_copy(
                groups[g].at[pl.ds(k * per, per)], tiles.at[g, pl.ds(k * per, per)], tile_sems.at[g, k]
            )
            for k in range(chunks)
        ]
        for g in range(3)
    ]
    load_x = pltpu.make_async_copy(x_hbm, x_ref, x_sem)

    @pl.when(part == 0)
    def _():
        for g in range(3):
            for k in range(chunks):
                moves[g][k].start()
        load_x.start()

    move[...] = halves_matrix(size, hubs)

    def clear(i, _):
        acc[i] = jnp.zeros((size, size), F32)
        return 0

    lax.fori_loop(0, acc.shape[0], clear, 0, unroll=4)

    off = 0
    for g in range(3):
        for k in range(chunks):

            @pl.when(part == 0)
            def _(move=moves[g][k]):
                move.wait()

            def add(i, _, g=g, k=k, off=off):
                t = k * per + i
                d = index[g][0][t]
                slot = d * wide + off + index[g][1][t]
                if parts > 1:
                    low = part * blocks
                    inside = jnp.logical_and(d >= low, d < low + blocks)
                    slot = jnp.where(inside, slot - low * wide, blocks * wide)
                acc[slot] += tiles[g, t].astype(F32)
                return 0

            lax.fori_loop(0, per, add, 0, unroll=4)
        off += cols[g]

    @pl.when(part == 0)
    def _():
        load_x.wait()

    def leave(b):
        rows = pl.ds(pl.multiple_of(b * size, size), size)
        there = pl.ds(pl.multiple_of((part * blocks + b) * size, size), size)
        return (
            pltpu.make_async_copy(al_ref.at[rows], al_hbm.at[there], out_sems.at[0, b]),
            pltpu.make_async_copy(bound_ref.at[rows], bound_hbm.at[there], out_sems.at[1, b]),
            pltpu.make_async_copy(other_ref.at[rows], other_hbm.at[there], out_sems.at[2, b]),
        )

    def finish(b, _):
        rows = pl.ds(pl.multiple_of(b * size, size), size)
        total = jnp.zeros((size, size), F32)
        for c in range(near):
            tile = acc[b * wide + c]
            total += tile
            ref, at = (al_ref, c) if c < cols[0] else (bound_ref, c - cols[0])
            ref[rows, at * size : (at + 1) * size] = tile.astype(BF16)
        for q in range(cols[2] // 2):
            pair = [acc[b * wide + near + 2 * q + i] for i in range(2)]
            total += pair[0] + pair[1]
            moved = dot(jnp.concatenate(pair, axis=1).astype(BF16), move[...]).astype(BF16)
            own_ref[rows, q * size : (q + 1) * size] = moved[:, :size]
            other_ref[rows, q * size : (q + 1) * size] = moved[:, size:]
        deg = 1.0 + jnp.sum(total, axis=1, keepdims=True)
        inv_ref[rows, :] = jnp.broadcast_to(1.0 / deg, (size, size))
        for copy in leave(b):
            copy.start()
        agg_ref[rows, :] = dot(al_ref[rows, :], x_ref[...])
        return 0

    lax.fori_loop(0, blocks, finish, 0)

    def end(b, _):
        for copy in leave(b):
            copy.wait()
        return 0

    lax.fori_loop(0, blocks, end, 0)


def cuts_of(rows, cuts):
    return [slice(k * rows // cuts, (k + 1) * rows // cuts) for k in range(cuts)]


def place(first, last, got_ref, dest_ref, start, lanes=slice(None)):
    per = last - first
    for o in range(got_ref.shape[0]):
        dest_ref[start + o * per : start + (o + 1) * per, lanes] = got_ref[o, first:last, :]


def stage_kernel(
    send_rows, parts, lists_hbm, hub_hbm, got_ref, agg_ref, own_ref, bound_in, other_in, sel_ref, sum_ref, *refs
):
    moved, (lists_ref, hub_ref, x_ref, sems) = refs[:-4], refs[-4:]
    part = pl.program_id(0)
    per = got_ref.shape[1]
    rows, bound = bound_in.shape if parts > 1 else moved[0].shape
    copies = fetch(((lists_hbm, lists_ref), (hub_hbm, hub_ref), *zip((bound_in, other_in), moved)), sems)

    @pl.when(part == 0)
    def _():
        place(0, send_rows, got_ref, x_ref, 0)
        place(send_rows, per, got_ref, x_ref, bound)

    for at in cuts_of(rows, 4):
        sum_ref[at, :] = agg_ref[at, :] + dot(own_ref[at, :], x_ref[bound:, :])
    copies[0].wait()
    copies[1].wait()

    @pl.when(part == 0)
    def _():
        fill_select(lists_ref, hub_ref, sel_ref)

    if moved:
        copies[2].wait()
    bound_ref = moved[0] if moved else bound_in
    for at in cuts_of(rows, 4):
        sum_ref[at, :] += dot(bound_ref[at, :], x_ref[0:bound, :])
    if moved:
        copies[3].wait()


def mean_kernel(send_rows, parts, got_ref, sum_ref, a_ref, inv_ref, sel_ref, mean_ref, send_ref, x_ref):
    part = pl.program_id(0)
    rows = a_ref.shape[0]

    @pl.when(part == 0)
    def _():
        place(send_rows, got_ref.shape[1], got_ref, x_ref, 0)

    for at in cuts_of(rows, 4):
        agg = sum_ref[at, :] + dot(a_ref[at, :], x_ref[...])
        there = pl.ds(pl.multiple_of(part * rows + at.start, rows // 4), rows // 4)
        mean_ref[there, :] = (agg * inv_ref[at, :]).astype(BF16)

    @pl.when(part == parts - 1)
    def _():
        fill_send(send_rows, sel_ref[...], mean_ref[...], send_ref)


def fill_first(both, weight, self_one, neigh_one, first):
    width = self_one.shape[0]
    weight[0:width, :] = self_one[...]
    weight[width : 2 * width, :] = neigh_one[...]
    first[...] = jnp.maximum(dot(both[...], weight[...]), 0.0).astype(BF16)


def own_kernel(
    send_rows,
    x_ref,
    mean_ref,
    got_one,
    got_two,
    local_ref,
    bound_ref,
    own_ref,
    self_one,
    neigh_one,
    self_two,
    sum_ref,
    part_ref,
    both,
    weight,
    first,
):
    part = pl.program_id(0)
    rows = local_ref.shape[0]
    nodes, width = x_ref.shape
    near = nodes + bound_ref.shape[1]

    @pl.when(part == 0)
    def _():
        both[0:nodes, 0:width] = x_ref[...]
        both[0:nodes, width : 2 * width] = mean_ref[...]
        for got_ref, lanes in ((got_one, slice(0, width)), (got_two, slice(width, 2 * width))):
            place(0, send_rows, got_ref, both, nodes, lanes)
            place(send_rows, got_ref.shape[1], got_ref, both, near, lanes)
        fill_first(both, weight, self_one, neigh_one, first)

    for at in cuts_of(rows, 4):
        sum_ref[at, :] = (
            dot(local_ref[at, :], first[0:nodes, :])
            + dot(bound_ref[at, :], first[nodes:near, :])
            + dot(own_ref[at, :], first[near:, :])
        )
    at = pl.ds(pl.multiple_of(part * rows, rows), rows)
    part_ref[...] = dot(first[at, :], self_two[...])


def last_kernel(
    send_rows,
    got_one,
    got_two,
    sum_ref,
    part_ref,
    inv_ref,
    a_ref,
    self_one,
    neigh_one,
    neigh_two,
    out_hbm,
    both,
    weight,
    first,
    mean_ref,
    out_ref,
    sems,
):
    part = pl.program_id(0)
    rows = a_ref.shape[0]
    width = self_one.shape[0]

    @pl.when(part == 0)
    def _():
        for got_ref, lanes in ((got_one, slice(0, width)), (got_two, slice(width, 2 * width))):
            place(send_rows, got_ref.shape[1], got_ref, both, 0, lanes)
        fill_first(both, weight, self_one, neigh_one, first)

    for at in cuts_of(rows, 4):
        agg = sum_ref[at, :] + dot(a_ref[at, :], first[...])
        inv = inv_ref[at, :]
        inv = jnp.concatenate([inv] * (agg.shape[1] // inv.shape[1]), axis=1)
        mean_ref[at, :] = (agg * inv).astype(BF16)
    outs = []
    for k, at in enumerate(cuts_of(rows, 4)):
        out_ref[at, :] = jnp.maximum(part_ref[at, :] + dot(mean_ref[at, :], neigh_two[...]), 0.0)
        there = pl.ds(pl.multiple_of(part * rows + at.start, rows // 4), rows // 4)
        outs.append(pltpu.make_async_copy(out_ref.at[at], out_hbm.at[there], sems.at[k]))
        outs[k].start()
    for copy in outs:
        copy.wait()


def per_device(
    features,
    send_lists,
    hub_rows,
    local_tiles,
    local_dst,
    local_src,
    remote_tiles,
    remote_dst,
    remote_src,
    hub_tiles,
    hub_dst,
    hub_src,
    self_one,
    neigh_one,
    self_two,
    neigh_two,
):
    nodes, f_in = features.shape
    hid = self_one.shape[1]
    tiles, size = local_tiles.shape[:2]
    _, peers, send_rows = send_lists.shape
    hubs = hub_rows.shape[0]
    per = send_rows + hubs // 2
    cols = (nodes // size, peers * send_rows // size, peers * hubs // size)
    wide = sum(cols)
    blocks = nodes // size
    parts = 1
    while blocks * wide * size * size * 4 > parts * 16 * MIB:
        parts *= 2
    rows = nodes // parts
    spare = 0 if parts == 1 else 1
    swap = [(i, i ^ 1) for i in range(peers)]
    sds = jax.ShapeDtypeStruct
    vm = whole()
    hbm = whole(pltpu.HBM)

    def split(width):
        return vm if parts == 1 else pl.BlockSpec((rows, width), lambda i, *_: (i, 0))

    dma = pltpu.SemaphoreType.DMA

    def in_hbm(*arrays):
        return [pltpu.with_memory_space_constraint(a, pltpu.HBM) for a in arrays]

    def kept(shape, dtype):
        return sds(shape, dtype) if parts > 1 else pltpu.VMEM(shape, dtype)

    lists = send_lists[0].T
    hub_row = hub_rows.reshape(1, hubs)
    chosen = peers * send_rows + hubs
    tables = [pltpu.VMEM((send_rows, peers), jnp.int32), pltpu.VMEM((1, hubs), jnp.int32)]
    send = pl.pallas_call(
        select_kernel,
        out_shape=kept((peers, per, f_in), BF16),
        in_specs=[hbm] * 3,
        out_specs=vm,
        scratch_shapes=[pltpu.VMEM((nodes, f_in), BF16), *tables, pltpu.VMEM((chosen, nodes), BF16), dma((3,))],
        compiler_params=params(16),
        name="select",
    )(*in_hbm(features, lists, hub_row))

    got = lax.all_to_all(send, "nodes", split_axis=0, concat_axis=0, tiled=True)

    chunks = 2
    bound = peers * send_rows
    other_rows = peers * (hubs // 2)
    a_local, a_bound, a_other, a_own, inv, agg = pl.pallas_call(
        functools.partial(build_kernel, cols, hubs, parts, chunks),
        out_shape=(
            pltpu.HBM((nodes, nodes), BF16),
            pltpu.HBM((nodes, bound), BF16),
            pltpu.HBM((nodes, other_rows), BF16),
            kept((nodes, other_rows), BF16),
            kept((nodes, size), F32),
            kept((nodes, f_in), F32),
        ),
        grid=(parts,),
        in_specs=[whole(pltpu.SMEM)] * 6 + [hbm] * 4,
        out_specs=(hbm, hbm, hbm, split(other_rows), split(size), split(f_in)),
        scratch_shapes=[
            pltpu.VMEM((blocks // parts * wide + spare, size, size), F32),
            pltpu.VMEM((3, tiles, size, size), BF16),
            pltpu.VMEM((nodes, f_in), BF16),
            pltpu.VMEM((2 * size, 2 * size), BF16),
            pltpu.VMEM((rows, nodes), BF16),
            pltpu.VMEM((rows, bound), BF16),
            pltpu.VMEM((rows, other_rows), BF16),
            dma((3, chunks)),
            dma(()),
            dma((3, blocks // parts)),
        ],
        compiler_params=params(36 if parts == 1 else 48),
        cost_estimate=pl.CostEstimate(flops=2 * nodes * nodes * f_in, bytes_accessed=40 * MIB, transcendentals=0),
        name="build",
    )(
        *in_hbm(local_dst, local_src, remote_dst, remote_src, hub_dst, hub_src),
        *in_hbm(features, local_tiles, remote_tiles, hub_tiles),
    )
    built = (got, a_local, a_bound, a_other, a_own, inv, agg)
    got, a_local, a_bound, a_other, a_own, inv, agg = lax.optimization_barrier(built)

    other = lax.ppermute(got, "nodes", swap)

    far = (a_bound, a_other)
    moved = far if parts == 1 else ()
    sel, agg, *moved = pl.pallas_call(
        functools.partial(stage_kernel, send_rows, parts),
        out_shape=(
            kept((chosen, nodes), BF16),
            kept((nodes, f_in), F32),
            *(kept(x.shape, x.dtype) for x in moved),
        ),
        grid=(parts,),
        in_specs=[hbm, hbm, vm, split(f_in), split(other_rows)]
        + ([hbm, hbm] if moved else [split(bound), whole(pl.ANY)]),
        out_specs=(vm, split(f_in), *([vm] * len(moved))),
        scratch_shapes=[*tables, pltpu.VMEM((bound + other_rows, f_in), BF16), dma((2 + len(moved),))],
        compiler_params=params(12 if parts == 1 else 32),
        cost_estimate=pl.CostEstimate(flops=0, bytes_accessed=8 * MIB, transcendentals=0),
        name="stage",
    )(*in_hbm(lists, hub_row), got, agg, a_own, *(in_hbm(*far) if moved else far))
    if moved:
        a_bound, a_other = moved

    mean, send = pl.pallas_call(
        functools.partial(mean_kernel, send_rows, parts),
        out_shape=(sds((nodes, f_in), BF16), sds(send.shape, BF16)),
        grid=(parts,),
        in_specs=[vm, split(f_in), split(other_rows), split(size), vm],
        out_specs=(vm, vm),
        scratch_shapes=[pltpu.VMEM((other_rows, f_in), BF16)],
        compiler_params=params(8 if parts == 1 else 48),
        name="mean",
    )(other, agg, a_other, inv, sel)

    got_two = lax.all_to_all(send, "nodes", split_axis=0, concat_axis=0, tiled=True)
    got_two, mean = lax.optimization_barrier((got_two, mean))
    other_two = lax.ppermute(got_two, "nodes", swap)

    near = nodes + bound + other_rows
    agg, part = pl.pallas_call(
        functools.partial(own_kernel, send_rows),
        out_shape=(sds((nodes, hid), F32), sds((nodes, hid), F32)),
        grid=(parts,),
        in_specs=[vm] * 4 + [split(nodes), split(bound), split(other_rows)] + [vm] * 3,
        out_specs=(split(hid), split(hid)),
        scratch_shapes=[
            pltpu.VMEM((near, 2 * f_in), BF16),
            pltpu.VMEM((2 * f_in, hid), BF16),
            pltpu.VMEM((near, hid), BF16),
        ],
        compiler_params=params(16 if parts == 1 else 48),
        cost_estimate=pl.CostEstimate(flops=2 * nodes * near * hid, bytes_accessed=8 * MIB, transcendentals=0),
        name="own",
    )(features, mean, got, got_two, a_local, a_bound, a_own, self_one, neigh_one, self_two)

    return pl.pallas_call(
        functools.partial(last_kernel, send_rows),
        out_shape=sds((nodes, hid), F32),
        grid=(parts,),
        in_specs=[vm] * 2 + [split(hid), split(hid), split(size), split(other_rows)] + [vm] * 3,
        out_specs=hbm,
        scratch_shapes=[
            pltpu.VMEM((other_rows, 2 * f_in), BF16),
            pltpu.VMEM((2 * f_in, hid), BF16),
            pltpu.VMEM((other_rows, hid), BF16),
            pltpu.VMEM((rows, hid), BF16),
            pltpu.VMEM((rows, hid), F32),
            dma((4,)),
        ],
        compiler_params=params(16 if parts == 1 else 56),
        name="last",
    )(other, other_two, agg, part, inv, a_other, self_one, neigh_one, neigh_two)


def solution(mesh):
    placed = (
        P("nodes", None),
        P("nodes", None, None),
        P("nodes"),
        P("nodes", None, None),
        P("nodes"),
        P("nodes"),
        P("nodes", None, None),
        P("nodes"),
        P("nodes"),
        P("nodes", None, None),
        P("nodes"),
        P("nodes"),
        P(),
        P(),
        P(),
        P(),
    )
    return jax.shard_map(
        per_device, mesh=mesh, in_specs=placed, out_specs=P("nodes", None), check_vma=False
    )
```

```python
import functools

import jax
import jax.numpy as jnp
from jax import lax
from jax.experimental import pallas as pl
from jax.experimental.pallas import tpu as pltpu
from jax.sharding import PartitionSpec as P

F32 = jnp.float32
BF16 = jnp.bfloat16
MIB = 1024 * 1024


def params(mib):
    return pltpu.CompilerParams(vmem_limit_bytes=mib * MIB)


def whole(memory=pltpu.VMEM):
    return pl.BlockSpec(memory_space=memory)


def dot(a, b):
    return jnp.dot(a, b, preferred_element_type=F32)


def fill_select(lists_ref, hub_ref, sel_ref):
    send_rows, peers = lists_ref.shape
    nodes = sel_ref.shape[1]
    hubs = hub_ref.shape[1]
    place = lax.broadcasted_iota(jnp.int32, (16, nodes), 1).astype(F32)

    def put(start, col):
        sel_ref[start : start + 16, :] = jnp.where(col == place, 1.0, 0.0).astype(BF16)

    lists = lists_ref[...].astype(F32)
    for p in range(peers):
        for c in range(0, send_rows, 16):
            put(p * send_rows + c, lists[c : c + 16, p : p + 1])
    table = jnp.broadcast_to(hub_ref[...].astype(F32), (16, hubs))
    sub = lax.broadcasted_iota(jnp.int32, (16, hubs), 0)
    lane = lax.broadcasted_iota(jnp.int32, (16, hubs), 1)
    for c in range(0, hubs, 16):
        picked = jnp.where(lane == sub + c, table, 0.0)
        put(peers * send_rows + c, jnp.sum(picked, axis=1, keepdims=True))


def fill_send(send_rows, sel, values, send_ref):
    peers = send_ref.shape[0]
    half = (sel.shape[0] - peers * send_rows) // 2
    rows = dot(sel, values).astype(BF16)
    for p in range(peers):
        send_ref[p, 0:send_rows, :] = rows[p * send_rows : (p + 1) * send_rows]
        start = peers * send_rows + half * (p % 2)
        send_ref[p, send_rows : send_rows + half, :] = rows[start : start + half]


def fetch(pairs, sems):
    copies = [pltpu.make_async_copy(src, dst, sems.at[i]) for i, (src, dst) in enumerate(pairs)]
    for copy in copies:
        copy.start()
    return copies


def select_kernel(x_hbm, lists_hbm, hub_hbm, send_ref, x_ref, lists_ref, hub_ref, sel_ref, sems):
    copies = fetch(((lists_hbm, lists_ref), (hub_hbm, hub_ref), (x_hbm, x_ref)), sems)
    copies[0].wait()
    copies[1].wait()
    fill_select(lists_ref, hub_ref, sel_ref)
    copies[2].wait()
    fill_send(lists_ref.shape[0], sel_ref[...], x_ref[...], send_ref)


def halves_matrix(size, hubs):
    half = hubs // 2
    shape = (2 * size, 2 * size)
    source = lax.broadcasted_iota(jnp.int32, shape, 0)
    target = lax.broadcasted_iota(jnp.int32, shape, 1)
    mine = lax.rem(lax.axis_index("nodes"), 2)
    inner = lax.rem(target, size)
    which = jnp.where(target < size, mine, 1 - mine)
    wanted = lax.div(inner, half) * hubs + which * half + lax.rem(inner, half)
    return jnp.where(source == wanted, 1.0, 0.0).astype(BF16)


def build_kernel(
    cols,
    hubs,
    parts,
    chunks,
    ld,
    ls,
    rd,
    rs,
    hd,
    hs,
    x_hbm,
    lt,
    rt,
    ht,
    al_hbm,
    bound_hbm,
    other_hbm,
    own_ref,
    inv_ref,
    agg_ref,
    acc,
    tiles,
    x_ref,
    move,
    al_ref,
    bound_ref,
    other_ref,
    tile_sems,
    x_sem,
    out_sems,
):
    part = pl.program_id(0)
    size = acc.shape[1]
    wide = sum(cols)
    near = cols[0] + cols[1]
    blocks = acc.shape[0] // wide
    count = lt.shape[0]
    per = count // chunks
    index = ((ld, ls), (rd, rs), (hd, hs))
    groups = (lt, rt, ht)
    moves = [
        [
            pltpu.make_async_copy(
                groups[g].at[pl.ds(k * per, per)], tiles.at[g, pl.ds(k * per, per)], tile_sems.at[g, k]
            )
            for k in range(chunks)
        ]
        for g in range(3)
    ]
    load_x = pltpu.make_async_copy(x_hbm, x_ref, x_sem)

    @pl.when(part == 0)
    def _():
        for g in range(3):
            for k in range(chunks):
                moves[g][k].start()
        load_x.start()

    move[...] = halves_matrix(size, hubs)

    def clear(i, _):
        acc[i] = jnp.zeros((size, size), F32)
        return 0

    lax.fori_loop(0, acc.shape[0], clear, 0, unroll=4)

    off = 0
    for g in range(3):
        for k in range(chunks):

            @pl.when(part == 0)
            def _(move=moves[g][k]):
                move.wait()

            def add(i, _, g=g, k=k, off=off):
                t = k * per + i
                d = index[g][0][t]
                slot = d * wide + off + index[g][1][t]
                if parts > 1:
                    low = part * blocks
                    inside = jnp.logical_and(d >= low, d < low + blocks)
                    slot = jnp.where(inside, slot - low * wide, blocks * wide)
                acc[slot] += tiles[g, t].astype(F32)
                return 0

            lax.fori_loop(0, per, add, 0, unroll=4)
        off += cols[g]

    @pl.when(part == 0)
    def _():
        load_x.wait()

    def leave(b):
        rows = pl.ds(pl.multiple_of(b * size, size), size)
        there = pl.ds(pl.multiple_of((part * blocks + b) * size, size), size)
        return (
            pltpu.make_async_copy(al_ref.at[rows], al_hbm.at[there], out_sems.at[0, b]),
            pltpu.make_async_copy(bound_ref.at[rows], bound_hbm.at[there], out_sems.at[1, b]),
            pltpu.make_async_copy(other_ref.at[rows], other_hbm.at[there], out_sems.at[2, b]),
        )

    def finish(b, _):
        rows = pl.ds(pl.multiple_of(b * size, size), size)
        total = jnp.zeros((size, size), F32)
        for c in range(near):
            tile = acc[b * wide + c]
            total += tile
            ref, at = (al_ref, c) if c < cols[0] else (bound_ref, c - cols[0])
            ref[rows, at * size : (at + 1) * size] = tile.astype(BF16)
        for q in range(cols[2] // 2):
            pair = [acc[b * wide + near + 2 * q + i] for i in range(2)]
            total += pair[0] + pair[1]
            moved = dot(jnp.concatenate(pair, axis=1).astype(BF16), move[...]).astype(BF16)
            own_ref[rows, q * size : (q + 1) * size] = moved[:, :size]
            other_ref[rows, q * size : (q + 1) * size] = moved[:, size:]
        deg = 1.0 + jnp.sum(total, axis=1, keepdims=True)
        inv_ref[rows, :] = jnp.broadcast_to(1.0 / deg, (size, size))
        for copy in leave(b):
            copy.start()
        agg_ref[rows, :] = dot(al_ref[rows, :], x_ref[...])
        return 0

    lax.fori_loop(0, blocks, finish, 0)

    def end(b, _):
        for copy in leave(b):
            copy.wait()
        return 0

    lax.fori_loop(0, blocks, end, 0)


def cuts_of(rows, cuts):
    return [slice(k * rows // cuts, (k + 1) * rows // cuts) for k in range(cuts)]


def place(first, last, got_ref, dest_ref, start, lanes=slice(None)):
    per = last - first
    for o in range(got_ref.shape[0]):
        dest_ref[start + o * per : start + (o + 1) * per, lanes] = got_ref[o, first:last, :]


def stage_kernel(
    send_rows, parts, lists_hbm, hub_hbm, got_ref, agg_ref, own_ref, bound_in, other_in, sel_ref, sum_ref, *refs
):
    moved, (lists_ref, hub_ref, x_ref, sems) = refs[:-4], refs[-4:]
    part = pl.program_id(0)
    per = got_ref.shape[1]
    rows, bound = bound_in.shape if parts > 1 else moved[0].shape
    copies = fetch(((lists_hbm, lists_ref), (hub_hbm, hub_ref), *zip((bound_in, other_in), moved)), sems)

    @pl.when(part == 0)
    def _():
        place(0, send_rows, got_ref, x_ref, 0)
        place(send_rows, per, got_ref, x_ref, bound)

    copies[0].wait()
    copies[1].wait()

    @pl.when(part == 0)
    def _():
        fill_select(lists_ref, hub_ref, sel_ref)

    if moved:
        copies[2].wait()
    bound_ref = moved[0] if moved else bound_in
    for at in cuts_of(rows, 4):
        total = dot(own_ref[at, :], x_ref[bound:, :]) + dot(bound_ref[at, :], x_ref[0:bound, :])
        sum_ref[at, :] = agg_ref[at, :] + total
    if moved:
        copies[3].wait()


def mean_kernel(send_rows, parts, got_ref, sum_ref, a_ref, inv_ref, sel_ref, mean_ref, send_ref, x_ref):
    part = pl.program_id(0)
    rows = a_ref.shape[0]

    @pl.when(part == 0)
    def _():
        place(send_rows, got_ref.shape[1], got_ref, x_ref, 0)

    for at in cuts_of(rows, 4):
        agg = sum_ref[at, :] + dot(a_ref[at, :], x_ref[...])
        there = pl.ds(pl.multiple_of(part * rows + at.start, rows // 4), rows // 4)
        mean_ref[there, :] = (agg * inv_ref[at, :]).astype(BF16)

    @pl.when(part == parts - 1)
    def _():
        fill_send(send_rows, sel_ref[...], mean_ref[...], send_ref)


def fill_first(both, weight, self_one, neigh_one, first):
    width = self_one.shape[0]
    weight[0:width, :] = self_one[...]
    weight[width : 2 * width, :] = neigh_one[...]
    first[...] = jnp.maximum(dot(both[...], weight[...]), 0.0).astype(BF16)


def own_kernel(
    send_rows,
    x_ref,
    mean_ref,
    got_one,
    got_two,
    local_ref,
    bound_ref,
    own_ref,
    self_one,
    neigh_one,
    self_two,
    sum_ref,
    part_ref,
    both,
    weight,
    first,
):
    part = pl.program_id(0)
    rows = local_ref.shape[0]
    nodes, width = x_ref.shape
    near = nodes + bound_ref.shape[1]

    @pl.when(part == 0)
    def _():
        both[0:nodes, 0:width] = x_ref[...]
        both[0:nodes, width : 2 * width] = mean_ref[...]
        for got_ref, lanes in ((got_one, slice(0, width)), (got_two, slice(width, 2 * width))):
            place(0, send_rows, got_ref, both, nodes, lanes)
            place(send_rows, got_ref.shape[1], got_ref, both, near, lanes)
        fill_first(both, weight, self_one, neigh_one, first)

    for at in cuts_of(rows, 4):
        sum_ref[at, :] = (
            dot(local_ref[at, :], first[0:nodes, :])
            + dot(bound_ref[at, :], first[nodes:near, :])
            + dot(own_ref[at, :], first[near:, :])
        )
    at = pl.ds(pl.multiple_of(part * rows, rows), rows)
    part_ref[...] = dot(first[at, :], self_two[...])


def last_kernel(
    send_rows,
    got_one,
    got_two,
    sum_ref,
    part_ref,
    inv_ref,
    a_ref,
    self_one,
    neigh_one,
    neigh_two,
    out_hbm,
    both,
    weight,
    first,
    mean_ref,
    out_ref,
    sems,
):
    part = pl.program_id(0)
    rows = a_ref.shape[0]
    width = self_one.shape[0]

    @pl.when(part == 0)
    def _():
        for got_ref, lanes in ((got_one, slice(0, width)), (got_two, slice(width, 2 * width))):
            place(send_rows, got_ref.shape[1], got_ref, both, 0, lanes)
        fill_first(both, weight, self_one, neigh_one, first)

    outs = []

    def leave(k, at):
        out_ref[at, :] = jnp.maximum(part_ref[at, :] + dot(mean_ref[at, :], neigh_two[...]), 0.0)
        there = pl.ds(pl.multiple_of(part * rows + at.start, rows // 4), rows // 4)
        outs.append(pltpu.make_async_copy(out_ref.at[at], out_hbm.at[there], sems.at[k]))
        outs[k].start()

    cuts = cuts_of(rows, 4)
    for k, at in enumerate(cuts):
        agg = sum_ref[at, :] + dot(a_ref[at, :], first[...])
        inv = inv_ref[at, :]
        inv = jnp.concatenate([inv] * (agg.shape[1] // inv.shape[1]), axis=1)
        mean_ref[at, :] = (agg * inv).astype(BF16)
        if k:
            leave(k - 1, cuts[k - 1])
    leave(3, cuts[3])
    for copy in outs:
        copy.wait()


def per_device(
    features,
    send_lists,
    hub_rows,
    local_tiles,
    local_dst,
    local_src,
    remote_tiles,
    remote_dst,
    remote_src,
    hub_tiles,
    hub_dst,
    hub_src,
    self_one,
    neigh_one,
    self_two,
    neigh_two,
):
    nodes, f_in = features.shape
    hid = self_one.shape[1]
    tiles, size = local_tiles.shape[:2]
    _, peers, send_rows = send_lists.shape
    hubs = hub_rows.shape[0]
    per = send_rows + hubs // 2
    cols = (nodes // size, peers * send_rows // size, peers * hubs // size)
    wide = sum(cols)
    blocks = nodes // size
    parts = 1
    while blocks * wide * size * size * 4 > parts * 16 * MIB:
        parts *= 2
    rows = nodes // parts
    spare = 0 if parts == 1 else 1
    swap = [(i, i ^ 1) for i in range(peers)]
    sds = jax.ShapeDtypeStruct
    vm = whole()
    hbm = whole(pltpu.HBM)

    def split(width):
        return vm if parts == 1 else pl.BlockSpec((rows, width), lambda i, *_: (i, 0))

    dma = pltpu.SemaphoreType.DMA

    def in_hbm(*arrays):
        return [pltpu.with_memory_space_constraint(a, pltpu.HBM) for a in arrays]

    def kept(shape, dtype):
        return sds(shape, dtype) if parts > 1 else pltpu.VMEM(shape, dtype)

    lists = send_lists[0].T
    hub_row = hub_rows.reshape(1, hubs)
    chosen = peers * send_rows + hubs
    tables = [pltpu.VMEM((send_rows, peers), jnp.int32), pltpu.VMEM((1, hubs), jnp.int32)]
    send = pl.pallas_call(
        select_kernel,
        out_shape=kept((peers, per, f_in), BF16),
        in_specs=[hbm] * 3,
        out_specs=vm,
        scratch_shapes=[pltpu.VMEM((nodes, f_in), BF16), *tables, pltpu.VMEM((chosen, nodes), BF16), dma((3,))],
        compiler_params=params(16),
        name="select",
    )(*in_hbm(features, lists, hub_row))

    got = lax.all_to_all(send, "nodes", split_axis=0, concat_axis=0, tiled=True)

    chunks = 2
    bound = peers * send_rows
    other_rows = peers * (hubs // 2)
    a_local, a_bound, a_other, a_own, inv, agg = pl.pallas_call(
        functools.partial(build_kernel, cols, hubs, parts, chunks),
        out_shape=(
            pltpu.HBM((nodes, nodes), BF16),
            pltpu.HBM((nodes, bound), BF16),
            pltpu.HBM((nodes, other_rows), BF16),
            kept((nodes, other_rows), BF16),
            kept((nodes, size), F32),
            kept((nodes, f_in), F32),
        ),
        grid=(parts,),
        in_specs=[whole(pltpu.SMEM)] * 6 + [hbm] * 4,
        out_specs=(hbm, hbm, hbm, split(other_rows), split(size), split(f_in)),
        scratch_shapes=[
            pltpu.VMEM((blocks // parts * wide + spare, size, size), F32),
            pltpu.VMEM((3, tiles, size, size), BF16),
            pltpu.VMEM((nodes, f_in), BF16),
            pltpu.VMEM((2 * size, 2 * size), BF16),
            pltpu.VMEM((rows, nodes), BF16),
            pltpu.VMEM((rows, bound), BF16),
            pltpu.VMEM((rows, other_rows), BF16),
            dma((3, chunks)),
            dma(()),
            dma((3, blocks // parts)),
        ],
        compiler_params=params(36 if parts == 1 else 48),
        cost_estimate=pl.CostEstimate(flops=2 * nodes * nodes * f_in, bytes_accessed=40 * MIB, transcendentals=0),
        name="build",
    )(
        *in_hbm(local_dst, local_src, remote_dst, remote_src, hub_dst, hub_src),
        *in_hbm(features, local_tiles, remote_tiles, hub_tiles),
    )
    built = (got, a_local, a_bound, a_other, a_own, inv, agg)
    got, a_local, a_bound, a_other, a_own, inv, agg = lax.optimization_barrier(built)

    other = lax.ppermute(got, "nodes", swap)

    far = (a_bound, a_other)
    moved = far if parts == 1 else ()
    sel, agg, *moved = pl.pallas_call(
        functools.partial(stage_kernel, send_rows, parts),
        out_shape=(
            kept((chosen, nodes), BF16),
            kept((nodes, f_in), F32),
            *(kept(x.shape, x.dtype) for x in moved),
        ),
        grid=(parts,),
        in_specs=[hbm, hbm, vm, split(f_in), split(other_rows)]
        + ([hbm, hbm] if moved else [split(bound), whole(pl.ANY)]),
        out_specs=(vm, split(f_in), *([vm] * len(moved))),
        scratch_shapes=[*tables, pltpu.VMEM((bound + other_rows, f_in), BF16), dma((2 + len(moved),))],
        compiler_params=params(12 if parts == 1 else 32),
        cost_estimate=pl.CostEstimate(flops=0, bytes_accessed=8 * MIB, transcendentals=0),
        name="stage",
    )(*in_hbm(lists, hub_row), got, agg, a_own, *(in_hbm(*far) if moved else far))
    if moved:
        a_bound, a_other = moved

    mean, send = pl.pallas_call(
        functools.partial(mean_kernel, send_rows, parts),
        out_shape=(sds((nodes, f_in), BF16), sds(send.shape, BF16)),
        grid=(parts,),
        in_specs=[vm, split(f_in), split(other_rows), split(size), vm],
        out_specs=(vm, vm),
        scratch_shapes=[pltpu.VMEM((other_rows, f_in), BF16)],
        compiler_params=params(8 if parts == 1 else 48),
        name="mean",
    )(other, agg, a_other, inv, sel)

    got_two = lax.all_to_all(send, "nodes", split_axis=0, concat_axis=0, tiled=True)
    got_two, mean = lax.optimization_barrier((got_two, mean))
    other_two = lax.ppermute(got_two, "nodes", swap)

    near = nodes + bound + other_rows
    agg, part = pl.pallas_call(
        functools.partial(own_kernel, send_rows),
        out_shape=(sds((nodes, hid), F32), sds((nodes, hid), F32)),
        grid=(parts,),
        in_specs=[vm] * 4 + [split(nodes), split(bound), split(other_rows)] + [vm] * 3,
        out_specs=(split(hid), split(hid)),
        scratch_shapes=[
            pltpu.VMEM((near, 2 * f_in), BF16),
            pltpu.VMEM((2 * f_in, hid), BF16),
            pltpu.VMEM((near, hid), BF16),
        ],
        compiler_params=params(16 if parts == 1 else 48),
        cost_estimate=pl.CostEstimate(flops=2 * nodes * near * hid, bytes_accessed=8 * MIB, transcendentals=0),
        name="own",
    )(features, mean, got, got_two, a_local, a_bound, a_own, self_one, neigh_one, self_two)

    return pl.pallas_call(
        functools.partial(last_kernel, send_rows),
        out_shape=sds((nodes, hid), F32),
        grid=(parts,),
        in_specs=[vm] * 2 + [split(hid), split(hid), split(size), split(other_rows)] + [vm] * 3,
        out_specs=hbm,
        scratch_shapes=[
            pltpu.VMEM((other_rows, 2 * f_in), BF16),
            pltpu.VMEM((2 * f_in, hid), BF16),
            pltpu.VMEM((other_rows, hid), BF16),
            pltpu.VMEM((rows, hid), BF16),
            pltpu.VMEM((rows, hid), F32),
            dma((4,)),
        ],
        compiler_params=params(16 if parts == 1 else 56),
        name="last",
    )(other, other_two, agg, part, inv, a_other, self_one, neigh_one, neigh_two)


def solution(mesh):
    placed = (
        P("nodes", None),
        P("nodes", None, None),
        P("nodes"),
        P("nodes", None, None),
        P("nodes"),
        P("nodes"),
        P("nodes", None, None),
        P("nodes"),
        P("nodes"),
        P("nodes", None, None),
        P("nodes"),
        P("nodes"),
        P(),
        P(),
        P(),
        P(),
    )
    return jax.shard_map(
        per_device, mesh=mesh, in_specs=placed, out_specs=P("nodes", None), check_vma=False
    )
```

```python
import functools

import jax
import jax.numpy as jnp
from jax import lax
from jax.experimental import pallas as pl
from jax.experimental.pallas import tpu as pltpu
from jax.sharding import PartitionSpec as P

F32 = jnp.float32
BF16 = jnp.bfloat16
MIB = 1024 * 1024


def params(mib):
    return pltpu.CompilerParams(vmem_limit_bytes=mib * MIB)


def whole(memory=pltpu.VMEM):
    return pl.BlockSpec(memory_space=memory)


def dot(a, b):
    return jnp.dot(a, b, preferred_element_type=F32)


def fill_select(lists_ref, hub_ref, sel_ref):
    send_rows, peers = lists_ref.shape
    nodes = sel_ref.shape[1]
    hubs = hub_ref.shape[1]
    place = lax.broadcasted_iota(jnp.int32, (16, nodes), 1).astype(F32)

    def put(start, col):
        sel_ref[start : start + 16, :] = jnp.where(col == place, 1.0, 0.0).astype(BF16)

    lists = lists_ref[...].astype(F32)
    for p in range(peers):
        for c in range(0, send_rows, 16):
            put(p * send_rows + c, lists[c : c + 16, p : p + 1])
    table = jnp.broadcast_to(hub_ref[...].astype(F32), (16, hubs))
    sub = lax.broadcasted_iota(jnp.int32, (16, hubs), 0)
    lane = lax.broadcasted_iota(jnp.int32, (16, hubs), 1)
    for c in range(0, hubs, 16):
        picked = jnp.where(lane == sub + c, table, 0.0)
        put(peers * send_rows + c, jnp.sum(picked, axis=1, keepdims=True))


def fill_send(send_rows, sel, values, send_ref):
    peers = send_ref.shape[0]
    half = (sel.shape[0] - peers * send_rows) // 2
    rows = dot(sel, values).astype(BF16)
    for p in range(peers):
        send_ref[p, 0:send_rows, :] = rows[p * send_rows : (p + 1) * send_rows]
        start = peers * send_rows + half * (p % 2)
        send_ref[p, send_rows : send_rows + half, :] = rows[start : start + half]


def fetch(pairs, sems):
    copies = [pltpu.make_async_copy(src, dst, sems.at[i]) for i, (src, dst) in enumerate(pairs)]
    for copy in copies:
        copy.start()
    return copies


def select_kernel(x_hbm, lists_hbm, hub_hbm, send_ref, x_ref, lists_ref, hub_ref, sel_ref, sems):
    copies = fetch(((lists_hbm, lists_ref), (hub_hbm, hub_ref), (x_hbm, x_ref)), sems)
    copies[0].wait()
    copies[1].wait()
    fill_select(lists_ref, hub_ref, sel_ref)
    copies[2].wait()
    fill_send(lists_ref.shape[0], sel_ref[...], x_ref[...], send_ref)


def halves_matrix(size, hubs):
    half = hubs // 2
    shape = (2 * size, 2 * size)
    source = lax.broadcasted_iota(jnp.int32, shape, 0)
    target = lax.broadcasted_iota(jnp.int32, shape, 1)
    mine = lax.rem(lax.axis_index("nodes"), 2)
    inner = lax.rem(target, size)
    which = jnp.where(target < size, mine, 1 - mine)
    wanted = lax.div(inner, half) * hubs + which * half + lax.rem(inner, half)
    return jnp.where(source == wanted, 1.0, 0.0).astype(BF16)


def build_kernel(
    cols,
    hubs,
    parts,
    chunks,
    ld,
    ls,
    rd,
    rs,
    hd,
    hs,
    x_hbm,
    lt,
    rt,
    ht,
    al_hbm,
    bound_hbm,
    other_hbm,
    inv_hbm,
    kept_ref,
    own_ref,
    agg_ref,
    acc,
    tiles,
    x_ref,
    move,
    al_ref,
    bound_ref,
    other_ref,
    inv_ref,
    tile_sems,
    x_sem,
    out_sems,
):
    part = pl.program_id(0)
    size = acc.shape[1]
    wide = sum(cols)
    near = cols[0] + cols[1]
    blocks = acc.shape[0] // wide
    count = lt.shape[0]
    per = count // chunks
    index = ((ld, ls), (rd, rs), (hd, hs))
    groups = (lt, rt, ht)
    moves = [
        [
            pltpu.make_async_copy(
                groups[g].at[pl.ds(k * per, per)], tiles.at[g, pl.ds(k * per, per)], tile_sems.at[g, k]
            )
            for k in range(chunks)
        ]
        for g in range(3)
    ]
    load_x = pltpu.make_async_copy(x_hbm, x_ref, x_sem)

    @pl.when(part == 0)
    def _():
        for g in range(3):
            for k in range(chunks):
                moves[g][k].start()
        load_x.start()

    move[...] = halves_matrix(size, hubs)

    def clear(i, _):
        acc[i] = jnp.zeros((size, size), F32)
        return 0

    lax.fori_loop(0, acc.shape[0], clear, 0, unroll=4)

    off = 0
    for g in range(3):
        for k in range(chunks):

            @pl.when(part == 0)
            def _(move=moves[g][k]):
                move.wait()

            def add(i, _, g=g, k=k, off=off):
                t = k * per + i
                d = index[g][0][t]
                slot = d * wide + off + index[g][1][t]
                if parts > 1:
                    low = part * blocks
                    inside = jnp.logical_and(d >= low, d < low + blocks)
                    slot = jnp.where(inside, slot - low * wide, blocks * wide)
                acc[slot] += tiles[g, t].astype(F32)
                return 0

            lax.fori_loop(0, per, add, 0, unroll=4)
        off += cols[g]

    @pl.when(part == 0)
    def _():
        load_x.wait()

    def leave(b):
        rows = pl.ds(pl.multiple_of(b * size, size), size)
        there = pl.ds(pl.multiple_of((part * blocks + b) * size, size), size)
        return (
            pltpu.make_async_copy(al_ref.at[rows], al_hbm.at[there], out_sems.at[0, b]),
            pltpu.make_async_copy(bound_ref.at[rows], bound_hbm.at[there], out_sems.at[1, b]),
            pltpu.make_async_copy(other_ref.at[rows], other_hbm.at[there], out_sems.at[2, b]),
            pltpu.make_async_copy(inv_ref.at[b], inv_hbm.at[part * blocks + b], out_sems.at[3, b]),
        )

    def finish(b, _):
        rows = pl.ds(pl.multiple_of(b * size, size), size)
        total = jnp.zeros((size, size), F32)
        for c in range(near):
            tile = acc[b * wide + c]
            total += tile
            if c < cols[0]:
                ref, at = al_ref, c
            elif c < cols[0] + cols[1] // 2:
                ref, at = kept_ref, c - cols[0]
            else:
                ref, at = bound_ref, c - cols[0] - cols[1] // 2
            ref[rows, at * size : (at + 1) * size] = tile.astype(BF16)
        for q in range(cols[2] // 2):
            pair = [acc[b * wide + near + 2 * q + i] for i in range(2)]
            total += pair[0] + pair[1]
            moved = dot(jnp.concatenate(pair, axis=1).astype(BF16), move[...]).astype(BF16)
            own_ref[rows, q * size : (q + 1) * size] = moved[:, :size]
            other_ref[rows, q * size : (q + 1) * size] = moved[:, size:]
        deg = 1.0 + jnp.sum(total, axis=1, keepdims=True)
        inv_ref[b] = jnp.broadcast_to(1.0 / deg, (size, size)).T[0:8, :]
        for copy in leave(b):
            copy.start()
        agg_ref[rows, :] = dot(al_ref[rows, :], x_ref[...])
        return 0

    lax.fori_loop(0, blocks, finish, 0)

    def end(b, _):
        for copy in leave(b):
            copy.wait()
        return 0

    lax.fori_loop(0, blocks, end, 0)


def cuts_of(rows, cuts):
    return [slice(k * rows // cuts, (k + 1) * rows // cuts) for k in range(cuts)]


def place(first, last, got_ref, dest_ref, start, lanes=slice(None)):
    per = last - first
    for o in range(got_ref.shape[0]):
        dest_ref[start + o * per : start + (o + 1) * per, lanes] = got_ref[o, first:last, :]


def stage_kernel(
    send_rows,
    parts,
    lists_hbm,
    hub_hbm,
    got_ref,
    inv_hbm,
    agg_ref,
    own_ref,
    kept_ref,
    bound_in,
    other_in,
    sel_ref,
    sum_ref,
    inv_ref,
    *refs,
):
    moved, (lists_ref, hub_ref, inv_row, x_ref, sems) = refs[:-5], refs[-5:]
    part = pl.program_id(0)
    per = got_ref.shape[1]
    rows, half = kept_ref.shape
    bound = 2 * half
    blocks, _, size = inv_row.shape
    inv_part = inv_hbm.at[pl.ds(part * blocks, blocks)]
    small = ((lists_hbm, lists_ref), (hub_hbm, hub_ref), (inv_part, inv_row))
    copies = fetch((*small, *zip((bound_in, other_in), moved)), sems)

    @pl.when(part == 0)
    def _():
        place(0, send_rows, got_ref, x_ref, 0)
        place(send_rows, per, got_ref, x_ref, bound)

    copies[0].wait()
    copies[1].wait()

    @pl.when(part == 0)
    def _():
        fill_select(lists_ref, hub_ref, sel_ref)

    copies[2].wait()
    for b in range(blocks):
        inv_ref[b * size : (b + 1) * size, :] = jnp.broadcast_to(inv_row[b, 0:1, :], (size, size)).T

    if moved:
        copies[3].wait()
    bound_ref = moved[0] if moved else bound_in
    for at in cuts_of(rows, 4):
        total = dot(own_ref[at, :], x_ref[bound:, :]) + dot(kept_ref[at, :], x_ref[0:half, :])
        total += dot(bound_ref[at, :], x_ref[half:bound, :])
        sum_ref[at, :] = agg_ref[at, :] + total
    if moved:
        copies[4].wait()


def mean_kernel(send_rows, parts, got_ref, sum_ref, a_ref, inv_ref, sel_ref, mean_ref, send_ref, x_ref):
    part = pl.program_id(0)
    rows = a_ref.shape[0]

    @pl.when(part == 0)
    def _():
        place(send_rows, got_ref.shape[1], got_ref, x_ref, 0)

    for at in cuts_of(rows, 4):
        agg = sum_ref[at, :] + dot(a_ref[at, :], x_ref[...])
        there = pl.ds(pl.multiple_of(part * rows + at.start, rows // 4), rows // 4)
        mean_ref[there, :] = (agg * inv_ref[at, :]).astype(BF16)

    @pl.when(part == parts - 1)
    def _():
        fill_send(send_rows, sel_ref[...], mean_ref[...], send_ref)


def fill_first(both, weight, self_one, neigh_one, first):
    width = self_one.shape[0]
    weight[0:width, :] = self_one[...]
    weight[width : 2 * width, :] = neigh_one[...]
    first[...] = jnp.maximum(dot(both[...], weight[...]), 0.0).astype(BF16)


def own_kernel(
    send_rows,
    x_ref,
    mean_ref,
    got_one,
    got_two,
    local_ref,
    kept_ref,
    bound_ref,
    own_ref,
    self_one,
    neigh_one,
    self_two,
    sum_ref,
    part_ref,
    both,
    weight,
    first,
):
    part = pl.program_id(0)
    rows = local_ref.shape[0]
    nodes, width = x_ref.shape
    middle = nodes + kept_ref.shape[1]
    near = middle + bound_ref.shape[1]

    @pl.when(part == 0)
    def _():
        both[0:nodes, 0:width] = x_ref[...]
        both[0:nodes, width : 2 * width] = mean_ref[...]
        for got_ref, lanes in ((got_one, slice(0, width)), (got_two, slice(width, 2 * width))):
            place(0, send_rows, got_ref, both, nodes, lanes)
            place(send_rows, got_ref.shape[1], got_ref, both, near, lanes)
        fill_first(both, weight, self_one, neigh_one, first)

    for at in cuts_of(rows, 4):
        sum_ref[at, :] = (
            dot(local_ref[at, :], first[0:nodes, :])
            + dot(kept_ref[at, :], first[nodes:middle, :])
            + dot(bound_ref[at, :], first[middle:near, :])
            + dot(own_ref[at, :], first[near:, :])
        )
    at = pl.ds(pl.multiple_of(part * rows, rows), rows)
    part_ref[...] = dot(first[at, :], self_two[...])


def last_kernel(
    send_rows,
    got_one,
    got_two,
    sum_ref,
    part_ref,
    inv_ref,
    a_ref,
    self_one,
    neigh_one,
    neigh_two,
    out_hbm,
    both,
    weight,
    first,
    mean_ref,
    out_ref,
    sems,
):
    part = pl.program_id(0)
    rows = a_ref.shape[0]
    width = self_one.shape[0]

    @pl.when(part == 0)
    def _():
        for got_ref, lanes in ((got_one, slice(0, width)), (got_two, slice(width, 2 * width))):
            place(send_rows, got_ref.shape[1], got_ref, both, 0, lanes)
        fill_first(both, weight, self_one, neigh_one, first)

    outs = []

    def leave(k, at):
        out_ref[at, :] = jnp.maximum(part_ref[at, :] + dot(mean_ref[at, :], neigh_two[...]), 0.0)
        there = pl.ds(pl.multiple_of(part * rows + at.start, rows // 4), rows // 4)
        outs.append(pltpu.make_async_copy(out_ref.at[at], out_hbm.at[there], sems.at[k]))
        outs[k].start()

    cuts = cuts_of(rows, 4)
    for k, at in enumerate(cuts):
        agg = sum_ref[at, :] + dot(a_ref[at, :], first[...])
        inv = inv_ref[at, :]
        inv = jnp.concatenate([inv] * (agg.shape[1] // inv.shape[1]), axis=1)
        mean_ref[at, :] = (agg * inv).astype(BF16)
        if k:
            leave(k - 1, cuts[k - 1])
    leave(3, cuts[3])
    for copy in outs:
        copy.wait()


def per_device(
    features,
    send_lists,
    hub_rows,
    local_tiles,
    local_dst,
    local_src,
    remote_tiles,
    remote_dst,
    remote_src,
    hub_tiles,
    hub_dst,
    hub_src,
    self_one,
    neigh_one,
    self_two,
    neigh_two,
):
    nodes, f_in = features.shape
    hid = self_one.shape[1]
    tiles, size = local_tiles.shape[:2]
    _, peers, send_rows = send_lists.shape
    hubs = hub_rows.shape[0]
    per = send_rows + hubs // 2
    cols = (nodes // size, peers * send_rows // size, peers * hubs // size)
    wide = sum(cols)
    blocks = nodes // size
    parts = 1
    while blocks * wide * size * size * 4 > parts * 16 * MIB:
        parts *= 2
    rows = nodes // parts
    spare = 0 if parts == 1 else 1
    swap = [(i, i ^ 1) for i in range(peers)]
    sds = jax.ShapeDtypeStruct
    vm = whole()
    hbm = whole(pltpu.HBM)

    def split(width):
        return vm if parts == 1 else pl.BlockSpec((rows, width), lambda i, *_: (i, 0))

    dma = pltpu.SemaphoreType.DMA

    def in_hbm(*arrays):
        return [pltpu.with_memory_space_constraint(a, pltpu.HBM) for a in arrays]

    def kept(shape, dtype):
        return sds(shape, dtype) if parts > 1 else pltpu.VMEM(shape, dtype)

    lists = send_lists[0].T
    hub_row = hub_rows.reshape(1, hubs)
    chosen = peers * send_rows + hubs
    tables = [pltpu.VMEM((send_rows, peers), jnp.int32), pltpu.VMEM((1, hubs), jnp.int32)]
    send = pl.pallas_call(
        select_kernel,
        out_shape=kept((peers, per, f_in), BF16),
        in_specs=[hbm] * 3,
        out_specs=vm,
        scratch_shapes=[pltpu.VMEM((nodes, f_in), BF16), *tables, pltpu.VMEM((chosen, nodes), BF16), dma((3,))],
        compiler_params=params(16),
        name="select",
    )(*in_hbm(features, lists, hub_row))

    got = lax.all_to_all(send, "nodes", split_axis=0, concat_axis=0, tiled=True)

    chunks = 2
    bound = peers * send_rows
    other_rows = peers * (hubs // 2)
    a_local, a_bound, a_other, inv, a_kept, a_own, agg = pl.pallas_call(
        functools.partial(build_kernel, cols, hubs, parts, chunks),
        out_shape=(
            pltpu.HBM((nodes, nodes), BF16),
            pltpu.HBM((nodes, bound // 2), BF16),
            pltpu.HBM((nodes, other_rows), BF16),
            pltpu.HBM((blocks, 8, size), F32),
            kept((nodes, bound // 2), BF16),
            kept((nodes, other_rows), BF16),
            kept((nodes, f_in), F32),
        ),
        grid=(parts,),
        in_specs=[whole(pltpu.SMEM)] * 6 + [hbm] * 4,
        out_specs=(hbm, hbm, hbm, hbm, split(bound // 2), split(other_rows), split(f_in)),
        scratch_shapes=[
            pltpu.VMEM((blocks // parts * wide + spare, size, size), F32),
            pltpu.VMEM((3, tiles, size, size), BF16),
            pltpu.VMEM((nodes, f_in), BF16),
            pltpu.VMEM((2 * size, 2 * size), BF16),
            pltpu.VMEM((rows, nodes), BF16),
            pltpu.VMEM((rows, bound // 2), BF16),
            pltpu.VMEM((rows, other_rows), BF16),
            pltpu.VMEM((blocks // parts, 8, size), F32),
            dma((3, chunks)),
            dma(()),
            dma((4, blocks // parts)),
        ],
        compiler_params=params(36 if parts == 1 else 48),
        cost_estimate=pl.CostEstimate(flops=2 * nodes * nodes * f_in, bytes_accessed=40 * MIB, transcendentals=0),
        name="build",
    )(
        *in_hbm(local_dst, local_src, remote_dst, remote_src, hub_dst, hub_src),
        *in_hbm(features, local_tiles, remote_tiles, hub_tiles),
    )
    built = (got, a_local, a_bound, a_other, inv, a_kept, a_own, agg)
    got, a_local, a_bound, a_other, inv, a_kept, a_own, agg = lax.optimization_barrier(built)

    other = lax.ppermute(got, "nodes", swap)

    far = (a_bound, a_other)
    moved = far if parts == 1 else ()
    sel, agg, inv, *moved = pl.pallas_call(
        functools.partial(stage_kernel, send_rows, parts),
        out_shape=(
            kept((chosen, nodes), BF16),
            kept((nodes, f_in), F32),
            kept((nodes, size), F32),
            *(kept(x.shape, x.dtype) for x in moved),
        ),
        grid=(parts,),
        in_specs=[hbm, hbm, vm, hbm, split(f_in), split(other_rows), split(bound // 2)]
        + ([hbm, hbm] if moved else [split(bound // 2), whole(pl.ANY)]),
        out_specs=(vm, split(f_in), split(size), *([vm] * len(moved))),
        scratch_shapes=[
            *tables,
            pltpu.VMEM((blocks // parts, 8, size), F32),
            pltpu.VMEM((bound + other_rows, f_in), BF16),
            dma((3 + len(moved),)),
        ],
        compiler_params=params(12 if parts == 1 else 32),
        cost_estimate=pl.CostEstimate(flops=0, bytes_accessed=8 * MIB, transcendentals=0),
        name="stage",
    )(*in_hbm(lists, hub_row), got, *in_hbm(inv), agg, a_own, a_kept, *(in_hbm(*far) if moved else far))
    if moved:
        a_bound, a_other = moved

    mean, send = pl.pallas_call(
        functools.partial(mean_kernel, send_rows, parts),
        out_shape=(sds((nodes, f_in), BF16), sds(send.shape, BF16)),
        grid=(parts,),
        in_specs=[vm, split(f_in), split(other_rows), split(size), vm],
        out_specs=(vm, vm),
        scratch_shapes=[pltpu.VMEM((other_rows, f_in), BF16)],
        compiler_params=params(8 if parts == 1 else 48),
        name="mean",
    )(other, agg, a_other, inv, sel)

    got_two = lax.all_to_all(send, "nodes", split_axis=0, concat_axis=0, tiled=True)
    got_two, mean = lax.optimization_barrier((got_two, mean))
    other_two = lax.ppermute(got_two, "nodes", swap)

    near = nodes + bound + other_rows
    agg, part = pl.pallas_call(
        functools.partial(own_kernel, send_rows),
        out_shape=(sds((nodes, hid), F32), sds((nodes, hid), F32)),
        grid=(parts,),
        in_specs=[vm] * 4 + [split(nodes), split(bound // 2), split(bound // 2), split(other_rows)] + [vm] * 3,
        out_specs=(split(hid), split(hid)),
        scratch_shapes=[
            pltpu.VMEM((near, 2 * f_in), BF16),
            pltpu.VMEM((2 * f_in, hid), BF16),
            pltpu.VMEM((near, hid), BF16),
        ],
        compiler_params=params(16 if parts == 1 else 48),
        cost_estimate=pl.CostEstimate(flops=2 * nodes * near * hid, bytes_accessed=8 * MIB, transcendentals=0),
        name="own",
    )(features, mean, got, got_two, a_local, a_kept, a_bound, a_own, self_one, neigh_one, self_two)

    return pl.pallas_call(
        functools.partial(last_kernel, send_rows),
        out_shape=sds((nodes, hid), F32),
        grid=(parts,),
        in_specs=[vm] * 2 + [split(hid), split(hid), split(size), split(other_rows)] + [vm] * 3,
        out_specs=hbm,
        scratch_shapes=[
            pltpu.VMEM((other_rows, 2 * f_in), BF16),
            pltpu.VMEM((2 * f_in, hid), BF16),
            pltpu.VMEM((other_rows, hid), BF16),
            pltpu.VMEM((rows, hid), BF16),
            pltpu.VMEM((rows, hid), F32),
            dma((4,)),
        ],
        compiler_params=params(16 if parts == 1 else 56),
        name="last",
    )(other, other_two, agg, part, inv, a_other, self_one, neigh_one, neigh_two)


def solution(mesh):
    placed = (
        P("nodes", None),
        P("nodes", None, None),
        P("nodes"),
        P("nodes", None, None),
        P("nodes"),
        P("nodes"),
        P("nodes", None, None),
        P("nodes"),
        P("nodes"),
        P("nodes", None, None),
        P("nodes"),
        P("nodes"),
        P(),
        P(),
        P(),
        P(),
    )
    return jax.shard_map(
        per_device, mesh=mesh, in_specs=placed, out_specs=P("nodes", None), check_vma=False
    )
```
